32 devices in a mesh: rep: 16 (over z, x, core), shard: 2 (over y).
Axes of the slice: x: 2, y: 2, z: 4, core: 2. Of those that a mesh axis runs over, the one named last changes fastest.
Arguments:
- activations: bfloat16 [2048, 1984], P('rep'), may hold values from -6 to 6
- out_grads: bfloat16 [2048, 496], P('rep', 'shard'), may hold values from -1.5 to 1.5
- error: bfloat16 [16, 1984, 496], P('rep', None, 'shard'), may hold values from -12 to 12
- momentum: bfloat16 [1984, 496], P(None, 'shard'), may hold values from -1.1953125 to 1.1953125
- query: float32 [496, 64], P('shard'), may hold values from -6 to 6
Outputs:
- error_new: bfloat16 [16, 1984, 496], P('rep', None, 'shard')
- momentum_new: bfloat16 [1984, 496], P(None, 'shard')
- query_new: float32 [496, 64], P('shard')
The draws below stay inside these ranges and needn't reach their ends.
All inputs are finite; a program needn't handle non-finite values.
Results may differ from the reference program's by a relative error of at most 0.001.
Values sent between devices are 32-bit elements; how exact they have to be, the bound alone decides.
A program may use at most 64 MiB of HBM per device.

```python
import jax
import jax.numpy as jnp
from jax import lax

D = 1984
RANK = 64
TOK_DEV = 128
TOKENS = 2048
COLS = 496
N_REP = 16


def block_scale(own_key, extent, shards, smallest, top_value):
    factor_of, own = 1.0, jax.random.fold_in(own_key, 6)
    for axis_at, blocks in shards:
        steps = jnp.exp(jax.random.uniform(jax.random.fold_in(own, axis_at), (blocks,), jnp.float32, smallest / len(shards), top_value / len(shards)))
        factor_of = factor_of * jnp.repeat(steps, extent[axis_at] // blocks).reshape([-1 if axis == axis_at else 1 for axis in range(len(extent))])
    return factor_of


def normal_values(key, extent, deviation, bound, pieces=(), kind=jnp.bfloat16):
    entries = deviation * jax.random.normal(key, extent, jnp.float32)
    if pieces:
        entries = entries * block_scale(key, extent, pieces, -0.22, 0.18)
    return jnp.clip(entries, -bound, bound).astype(kind)


def setup_inputs(seed: int = 0) -> dict:
    splits = jax.random.split(jax.random.key(seed), 6)
    activations = normal_values(splits[0], (TOKENS, D), 1.0, 6.0, ((0, 16),))
    out_grads = normal_values(splits[1], (TOKENS, COLS), 0.25, 1.5, ((0, 16), (1, 2)))
    error = normal_values(splits[2], (N_REP, D, COLS), 2.0, 12.0, ((0, 16), (2, 2)))
    momentum = normal_values(splits[3], (D, COLS), 0.2, 1.1953125, ((1, 2),))
    query = normal_values(splits[4], (COLS, RANK), 1.0, 6.0, ((0, 2),), jnp.float32)
    return {"activations": activations, "out_grads": out_grads, "error": error, "momentum": momentum, "query": query}


def merged_block(act_rows, grad_rows, err_block):
    grad = jnp.dot(act_rows.T.astype(jnp.float32), grad_rows.astype(jnp.float32), preferred_element_type=jnp.float32)
    return grad + err_block.astype(jnp.float32)

def reference(activations, out_grads, error, momentum, query):
    acts = activations.reshape(N_REP, TOK_DEV, D)
    grads = out_grads.reshape(N_REP, TOK_DEV, COLS)
    steps_idx = jnp.arange(N_REP).astype(jnp.int32)

    def add_factor(total, index):
        merged = merged_block(acts[index], grads[index], error[index])
        return (total + jnp.dot(merged, query, precision=lax.Precision.HIGHEST), None)
    factor, unused = lax.scan(add_factor, jnp.zeros((D, RANK), jnp.float32), steps_idx)
    gram = jnp.dot(factor.T, factor, precision=lax.Precision.HIGHEST)
    lower = jnp.linalg.cholesky(gram)
    basis = jax.scipy.linalg.solve_triangular(lower, factor.T, lower=True).T

    def add_query(total, index):
        merged = merged_block(acts[index], grads[index], error[index])
        return (total + jnp.dot(merged.T, basis, precision=lax.Precision.HIGHEST), None)
    qsum, unused = lax.scan(add_query, jnp.zeros((COLS, RANK), jnp.float32), steps_idx)
    query_new = qsum / N_REP
    approx = jnp.dot(basis, query_new.T, precision=lax.Precision.HIGHEST)

    def new_error(index):
        merged = merged_block(acts[index], grads[index], error[index])
        return (merged - approx).astype(jnp.bfloat16)
    error_new = lax.map(new_error, steps_idx)
    momentum_new = (0.9 * momentum.astype(jnp.float32) + approx).astype(jnp.bfloat16)
    return (error_new, momentum_new, query_new)
```

```python
import functools

import jax
import jax.numpy as jnp
from jax import lax
from jax.experimental import pallas as pl
from jax.experimental.pallas import tpu as pltpu
from jax.sharding import PartitionSpec as P

MESH = pl.DeviceIdType.MESH
F32 = jnp.float32
BF16 = jnp.bfloat16
NN = (((1,), (0,)), ((), ()))
NT = (((1,), (1,)), ((), ()))
TN = (((0,), (0,)), ((), ()))


def up(value, step):
    return -(-value // step) * step


def dot(a, b, dims=NN):
    return lax.dot_general(a, b, dims, preferred_element_type=F32)


def exact(a, b, dims=NN):
    return lax.dot_general(
        a, b, dims, preferred_element_type=F32, precision=lax.Precision.HIGHEST
    )


def split(x):
    high = x.astype(BF16)
    return high, (x - high.astype(F32)).astype(BF16)


def each(first, last, body):
    if last - first <= 16:
        for t in range(first, last):
            body(t)
    else:
        lax.fori_loop(first, last, lambda t, c: (body(t), c)[1], 0)


def phases_of(n_rep, n_shard):
    core = 2 if n_rep % 2 == 0 else 1
    mid = 2 if n_rep % (2 * core) == 0 else 1
    high = n_rep // (core * mid)
    return core, mid, high


def phases_here(n_rep, n_shard):
    core_n, mid_n, high_n = phases_of(n_rep, n_shard)
    rep = lax.axis_index("rep")
    shard = lax.axis_index("shard")
    core = rep % core_n
    mid = (rep // core_n) % mid_n
    high = rep // (core_n * mid_n)
    low = core_n * mid_n
    return (
        (core_n, core, lambda d: (rep - core + d, shard)),
        (
            mid_n * n_shard,
            mid * n_shard + shard,
            lambda d: (high * low + (d // n_shard) * core_n + core, d % n_shard),
        ),
        (high_n, high, lambda d: (d * low + mid * core_n + core, shard)),
    )


def inverse_factor(aug, rank):
    blocks = [aug[8 * v : 8 * v + 8] for v in range(rank // 8)]
    lanes = blocks[0].shape[1]
    sub = lax.broadcasted_iota(jnp.int32, (8, lanes), 0)
    done = []
    for at in range(rank // 8):
        head = blocks[at]
        below = blocks[at + 1 :]
        cols = [
            [jnp.broadcast_to(x[:, 8 * at + k : 8 * at + k + 1], (8, lanes)) for x in [head] + below]
            for k in range(8)
        ]
        pivots = jnp.ones((8, lanes), F32)
        for k in range(8):
            pivot = cols[k][0][k : k + 1]
            inv = 1.0 / pivot
            pivots = jnp.where(sub == k, pivot, pivots)
            row = head[k : k + 1] * inv
            for m in range(k + 1, 8):
                ratio = cols[m][0][k : k + 1] * inv
                for v in range(len(below) + 1):
                    cols[m][v] = cols[m][v] - cols[k][v] * ratio
            head = head - jnp.where(sub > k, cols[k][0], 0.0) * row
            below = [x - cols[k][v + 1] * row for v, x in enumerate(below)]
        done.append(head * lax.rsqrt(pivots))
        blocks[at + 1 :] = below
    return jnp.concatenate(done, axis=0)


def kernel(
    n_rep, n_shard, rows_q,
    act_ref, out_ref, err_ref, mom_ref, query_ref,
    err_new_ref, mom_new_ref, query_new_ref,
    at_ref, merged_ref, part_ref, factor_ref, land0, land1, land2,
    sq_ref, lq_ref, rq_ref,
    send_f, recv_f, send_g, recv_g, send_q, recv_q, send_h, recv_h,
):
    depth, cols = err_ref.shape
    rank = query_ref.shape[1]
    half = up(-(-depth // 2), 128)
    rest = depth - half
    wide = 2 * rank
    phases = phases_here(n_rep, n_shard)
    lands = (land0, land1, land2)
    rep = lax.axis_index("rep")
    shard = lax.axis_index("shard")
    core_n, mid_n, high_n = phases_of(n_rep, n_shard)

    barrier = pltpu.get_barrier_semaphore()

    def greet_rep(t):
        pl.semaphore_signal(
            barrier, inc=1, device_id=((rep + t) % n_rep, shard), device_id_type=MESH
        )

    def greet_shard(t):
        _, digit, peer = phases[1]
        mid, other = t // (n_shard - 1), t % (n_shard - 1)
        to = mid * n_shard + (shard + 1 + other) % n_shard
        pl.semaphore_signal(barrier, inc=1, device_id=peer(to), device_id_type=MESH)

    each(1, n_rep, greet_rep)
    across = mid_n * (n_shard - 1)
    if across:
        each(0, across, greet_shard)

    query = query_ref[...]
    none = jnp.zeros_like(query)
    q_top = jnp.concatenate(split(jnp.concatenate([query, none], axis=1)), axis=1)
    q_bot = jnp.concatenate(split(jnp.concatenate([none, query], axis=1)), axis=1)
    out_grads = out_ref[...]
    at_ref[...] = act_ref[...].T

    def partial(first, size, q):
        gq = dot(out_grads, q)
        gq = jnp.concatenate(split(gq[:, :wide] + gq[:, wide:]), axis=1)
        both = dot(err_ref[first : first + size], q) + dot(at_ref[first : first + size], gq)
        return both[:, :wide] + both[:, wide:]

    top = partial(0, half, q_top)
    bot = partial(half, rest, q_bot)
    part_ref[:rest] = top[:rest] + bot
    part_ref[rest:half] = top[rest:]
    if part_ref.shape[0] > half:
        part_ref[half:] = jnp.zeros((part_ref.shape[0] - half, wide), F32)

    pl.semaphore_wait(barrier, n_rep - 1 + across)

    base, size = 0, part_ref.shape[0]
    bases = []
    first_sem = 0
    for k, (count, digit, peer) in enumerate(phases):
        size = size // count
        land = lands[k]

        def copy(t, base=base, size=size, count=count, digit=digit, peer=peer, land=land, s0=first_sem):
            to = (digit + t) % count
            return pltpu.make_async_remote_copy(
                src_ref=part_ref.at[pl.ds(pl.multiple_of(base + to * size, 8), size)],
                dst_ref=land.at[t],
                send_sem=send_f.at[s0 + t],
                recv_sem=recv_f.at[s0 + t],
                device_id=peer(to),
                device_id_type=MESH,
            )

        each(1, count, lambda t: copy(t).start())
        if k == 0:
            for first, rows in ((0, half), (half, rest)):
                merged_ref[first : first + rows] = dot(
                    at_ref[first : first + rows], out_grads
                ) + err_ref[first : first + rows].astype(F32)
        each(1, count, lambda t: copy(t).wait())
        base = base + digit * size
        bases.append((base, size, first_sem))
        mine = pl.ds(pl.multiple_of(base, 8), size)
        total = part_ref[mine]
        if count <= 16:
            for t in range(1, count):
                total = total + land[t]
        else:
            total = lax.fori_loop(1, count, lambda t, x: x + land[t], total)
        if k < len(phases) - 1:
            part_ref[mine] = total
        else:
            factor_ref[mine] = total
        first_sem += count

    for k in reversed(range(len(phases))):
        count, digit, peer = phases[k]
        base, size, s0 = bases[k]

        def back(t, base=base, size=size, count=count, digit=digit, peer=peer, s0=s0):
            mine = pl.ds(pl.multiple_of(base, 8), size)
            return pltpu.make_async_remote_copy(
                src_ref=factor_ref.at[mine],
                dst_ref=factor_ref.at[mine],
                send_sem=send_g.at[s0 + t],
                recv_sem=recv_g.at[s0 + t],
                device_id=peer((digit + t) % count),
                device_id_type=MESH,
            )

        def arrive(t, base=base, size=size, count=count, digit=digit, peer=peer, s0=s0):
            whole = base - digit * size
            owner = (digit - t + count) % count
            theirs = pl.ds(pl.multiple_of(whole + owner * size, 8), size)
            pltpu.make_async_remote_copy(
                src_ref=factor_ref.at[theirs],
                dst_ref=factor_ref.at[theirs],
                send_sem=send_g.at[s0 + t],
                recv_sem=recv_g.at[s0 + t],
                device_id=peer((digit + t) % count),
                device_id_type=MESH,
            ).wait_recv()

        each(1, count, lambda t: back(t).start())
        each(1, count, lambda t: back(t).wait_send())
        each(1, count, arrive)

    factor = factor_ref[:half]
    high, low = split(factor)
    pair = jnp.concatenate([high, low], axis=1)
    pair_t = pair.T

    ft_top = jnp.concatenate([pair_t[:rank], pair_t[wide : wide + rank]], axis=0)
    ft_bot = jnp.concatenate([pair_t[rank:wide], pair_t[wide + rank :]], axis=0)[:, :rest]
    af = dot(ft_top, act_ref[:, :half], NT) + dot(ft_bot, act_ref[:, half:], NT)
    af = jnp.concatenate(split(af[:rank] + af[rank:]), axis=0)
    local = dot(ft_top, err_ref[:half]) + dot(ft_bot, err_ref[half:]) + dot(af, out_grads)
    local = local[:rank] + local[rank:]
    lane_blocks = up(cols, 128) // 128
    for b in range(lane_blocks):
        here = min(128, cols - 128 * b)
        sq_ref[b * rank : (b + 1) * rank, :here] = local[:, 128 * b : 128 * b + here]
        if here < 128:
            sq_ref[b * rank : (b + 1) * rank, here:] = jnp.zeros((rank, 128 - here), F32)
    if sq_ref.shape[0] > lane_blocks * rank:
        sq_ref[lane_blocks * rank :] = jnp.zeros((sq_ref.shape[0] - lane_blocks * rank, 128), F32)

    def scatter(t):
        to = (rep + t) % n_rep
        return pltpu.make_async_remote_copy(
            src_ref=sq_ref.at[pl.ds(pl.multiple_of(to * rows_q, 8), rows_q)],
            dst_ref=lq_ref.at[t],
            send_sem=send_q.at[t],
            recv_sem=recv_q.at[t],
            device_id=(to, shard),
            device_id_type=MESH,
        )

    each(1, n_rep, lambda t: scatter(t).start())

    prod = dot(pair_t, pair)
    g1 = prod[:rank] + prod[wide : wide + rank]
    g2 = prod[rank:wide] + prod[wide + rank :]
    g1 = g1[:, :wide] + g1[:, wide:]
    g2 = g2[:, :wide] + g2[:, wide:]
    gram = g1 + pltpu.roll(g2, rank, 1)
    lane = lax.broadcasted_iota(jnp.int32, (rank, wide), 1)
    row = lax.broadcasted_iota(jnp.int32, (rank, wide), 0)
    aug = jnp.where(lane < rank, gram, jnp.where(lane - rank == row, 1.0, 0.0))

    each(1, n_rep, lambda t: scatter(t).wait())
    mine_q = pl.ds(pl.multiple_of(rep * rows_q, 8), rows_q)
    total = sq_ref[mine_q]
    if n_rep <= 16:
        for t in range(1, n_rep):
            total = total + lq_ref[t]
    else:
        total = lax.fori_loop(1, n_rep, lambda t, x: x + lq_ref[t], total)
    rq_ref[mine_q] = total / n_rep

    def gather(t, owner):
        theirs = pl.ds(pl.multiple_of(owner * rows_q, 8), rows_q)
        return pltpu.make_async_remote_copy(
            src_ref=rq_ref.at[theirs],
            dst_ref=rq_ref.at[theirs],
            send_sem=send_h.at[t],
            recv_sem=recv_h.at[t],
            device_id=((rep + t) % n_rep, shard),
            device_id_type=MESH,
        )

    each(1, n_rep, lambda t: gather(t, rep).start())

    inverse = inverse_factor(aug, rank)
    inverse = pltpu.roll(inverse, rank, 1)[:, :rank]

    each(1, n_rep, lambda t: gather(t, rep).wait_send())
    each(1, n_rep, lambda t: gather(t, (rep - t + n_rep) % n_rep).wait_recv())

    summed = jnp.concatenate(
        [rq_ref[b * rank : (b + 1) * rank] for b in range(lane_blocks)], axis=1
    )
    right_t = exact(inverse, summed)
    query_new_ref[...] = right_t.T[:cols]
    mixed = exact(inverse, right_t, TN)[:, :cols]
    m_high, m_low = split(mixed)
    gap = jnp.zeros_like(m_high)
    pair = jnp.concatenate(split(factor_ref[:half]), axis=1)

    for first, rows, on_high, on_low in (
        (0, half, [m_high, gap, m_high, gap], [m_low, gap]),
        (half, rest, [gap, m_high, gap, m_high], [gap, m_low]),
    ):
        approx = dot(pair[:rows], jnp.concatenate(on_high, axis=0)) + dot(
            pair[:rows, :wide], jnp.concatenate(on_low, axis=0)
        )
        at = slice(first, first + rows)
        err_new_ref[at] = (merged_ref[at] - approx).astype(BF16)
        mom_new_ref[at] = (0.9 * mom_ref[at].astype(F32) + approx).astype(BF16)


def step(n_rep, n_shard, activations, out_grads, error, momentum, query):
    _, depth, cols = error.shape
    rank = query.shape[1]
    tokens = activations.shape[0]
    half = up(-(-depth // 2), 128)
    devices = n_rep * n_shard
    padded = up(half, 8 * devices)
    core_n, mid_n, high_n = phases_of(n_rep, n_shard)
    counts = (core_n, mid_n * n_shard, high_n)
    lane_blocks = up(cols, 128) // 128
    rows_q = up(lane_blocks * rank, 8 * n_rep) // n_rep
    sizes, size = [], padded
    for count in counts:
        size //= count
        sizes.append(size)
    dma = pltpu.SemaphoreType.DMA
    err_new, mom_new, query_new = pl.pallas_call(
        functools.partial(kernel, n_rep, n_shard, rows_q),
        out_shape=(
            jax.ShapeDtypeStruct((depth, cols), BF16),
            jax.ShapeDtypeStruct((depth, cols), BF16),
            jax.ShapeDtypeStruct((cols, rank), F32),
        ),
        in_specs=[pl.BlockSpec(memory_space=pltpu.VMEM)] * 5,
        out_specs=[pl.BlockSpec(memory_space=pltpu.VMEM)] * 3,
        scratch_shapes=[
            pltpu.VMEM((depth, tokens), BF16),
            pltpu.VMEM((depth, cols), F32),
            pltpu.VMEM((padded, 2 * rank), F32),
            pltpu.VMEM((padded, 2 * rank), F32),
        ]
        + [pltpu.VMEM((c, s, 2 * rank), F32) for c, s in zip(counts, sizes)]
        + [
            pltpu.VMEM((rows_q * n_rep, 128), F32),
            pltpu.VMEM((n_rep, rows_q, 128), F32),
            pltpu.VMEM((rows_q * n_rep, 128), F32),
        ]
        + [dma((sum(counts),))] * 4
        + [dma((n_rep,))] * 4,
        compiler_params=pltpu.CompilerParams(
            collective_id=0, has_side_effects=True, vmem_limit_bytes=48 * 1024 * 1024
        ),
    )(activations, out_grads, error.reshape(depth, cols), momentum, query)
    return err_new[None], mom_new, query_new


def solution(mesh):
    return jax.shard_map(
        functools.partial(step, mesh.shape["rep"], mesh.shape["shard"]),
        mesh=mesh,
        in_specs=(
            P("rep", None),
            P("rep", "shard"),
            P("rep", None, "shard"),
            P(None, "shard"),
            P("shard", None),
        ),
        out_specs=(P("rep", None, "shard"), P(None, "shard"), P("shard", None)),
        check_vma=False,
    )
```

```python
import functools

import jax
import jax.numpy as jnp
from jax import lax
from jax.experimental import pallas as pl
from jax.experimental.pallas import tpu as pltpu
from jax.sharding import PartitionSpec as P

MESH = pl.DeviceIdType.MESH
F32 = jnp.float32
BF16 = jnp.bfloat16
NN = (((1,), (0,)), ((), ()))
NT = (((1,), (1,)), ((), ()))
TN = (((0,), (0,)), ((), ()))


def up(value, step):
    return -(-value // step) * step


def dot(a, b, dims=NN):
    return lax.dot_general(a, b, dims, preferred_element_type=F32)


def exact(a, b, dims=NN):
    return lax.dot_general(
        a, b, dims, preferred_element_type=F32, precision=lax.Precision.HIGHEST
    )


def split(x):
    high = x.astype(BF16)
    return high, (x - high.astype(F32)).astype(BF16)


def each(first, last, body):
    if last - first <= 16:
        for t in range(first, last):
            body(t)
    else:
        lax.fori_loop(first, last, lambda t, c: (body(t), c)[1], 0)


def phases_of(n_rep, n_shard):
    core = 2 if n_rep % 2 == 0 else 1
    mid = 2 if n_rep % (2 * core) == 0 else 1
    high = n_rep // (core * mid)
    return core, mid, high


def phases_here(n_rep, n_shard):
    core_n, mid_n, high_n = phases_of(n_rep, n_shard)
    rep = lax.axis_index("rep")
    shard = lax.axis_index("shard")
    core = rep % core_n
    mid = (rep // core_n) % mid_n
    high = rep // (core_n * mid_n)
    low = core_n * mid_n
    return (
        (core_n, core, lambda d: (rep - core + d, shard)),
        (
            mid_n * n_shard,
            mid * n_shard + shard,
            lambda d: (high * low + (d // n_shard) * core_n + core, d % n_shard),
        ),
        (high_n, high, lambda d: (d * low + mid * core_n + core, shard)),
    )


def eliminate(blocks, done, first, last):
    lanes = blocks[0].shape[1]
    sub = lax.broadcasted_iota(jnp.int32, (8, lanes), 0)
    for at in range(first, last):
        head = blocks[at]
        below = blocks[at + 1 :]
        cols = [
            [jnp.broadcast_to(x[:, 8 * at + k : 8 * at + k + 1], (8, lanes)) for x in [head] + below]
            for k in range(8)
        ]
        pivots = jnp.ones((8, lanes), F32)
        for k in range(8):
            pivot = cols[k][0][k : k + 1]
            inv = 1.0 / pivot
            pivots = jnp.where(sub == k, pivot, pivots)
            row = head[k : k + 1] * inv
            for m in range(k + 1, 8):
                ratio = cols[m][0][k : k + 1] * inv
                for v in range(len(below) + 1):
                    cols[m][v] = cols[m][v] - cols[k][v] * ratio
            head = head - jnp.where(sub > k, cols[k][0], 0.0) * row
            below = [x - cols[k][v + 1] * row for v, x in enumerate(below)]
        done.append(head * lax.rsqrt(pivots))
        blocks[at + 1 :] = below


def kernel(
    n_rep, n_shard, rows_q,
    act_hbm, out_hbm, err_hbm, query_hbm,
    pair_ref, merged_ref, mixed_ref, right_ref,
    at_ref, gt_ref, err_ref, query_ref, part_ref, factor_ref, land0, land1, land2,
    sq_ref, lq_ref, rq_ref,
    in_sem, send_f, recv_f, send_g, recv_g, send_q, recv_q, send_h, recv_h,
):
    depth, cols = err_hbm.shape
    rank = query_ref.shape[0]
    half = part_ref.shape[0]
    wide = 2 * rank
    phases = phases_here(n_rep, n_shard)
    lands = (land0, land1, land2)
    rep = lax.axis_index("rep")
    shard = lax.axis_index("shard")
    core_n, mid_n, high_n = phases_of(n_rep, n_shard)

    cut = up(-(-depth // 2), 16)
    loads = [
        pltpu.make_async_copy(src, dst, in_sem.at[i])
        for i, (src, dst) in enumerate((
            (query_hbm, query_ref),
            (out_hbm, gt_ref),
            (err_hbm.at[:cut], err_ref.at[:cut]),
            (err_hbm.at[cut:], err_ref.at[cut:depth]),
            (act_hbm, at_ref.at[:depth]),
        ))
    ]
    for load in loads:
        load.start()

    barrier = pltpu.get_barrier_semaphore()

    def greet_rep(t):
        pl.semaphore_signal(
            barrier, inc=1, device_id=((rep + t) % n_rep, shard), device_id_type=MESH
        )

    def greet_shard(t):
        _, digit, peer = phases[1]
        mid, other = t // (n_shard - 1), t % (n_shard - 1)
        to = mid * n_shard + (shard + 1 + other) % n_shard
        pl.semaphore_signal(barrier, inc=1, device_id=peer(to), device_id_type=MESH)

    each(1, n_rep, greet_rep)
    across = mid_n * (n_shard - 1)
    if across:
        each(0, across, greet_shard)

    if 2 * half > depth:
        err_ref[depth:] = jnp.zeros((2 * half - depth, cols), BF16)
        at_ref[depth:] = jnp.zeros((2 * half - depth, at_ref.shape[1]), BF16)

    loads[0].wait()
    loads[1].wait()
    query = query_ref[...]
    none = jnp.zeros_like(query)
    q_top = jnp.concatenate(split(jnp.concatenate([query, none], axis=0)), axis=0)
    q_bot = jnp.concatenate(split(jnp.concatenate([none, query], axis=0)), axis=0)

    def through(q):
        gq = dot(q, gt_ref[...])
        return jnp.concatenate(split(gq[:wide] + gq[wide:]), axis=0)

    gq_top, gq_bot = through(q_top), through(q_bot)
    for load in loads[2:]:
        load.wait()

    def rows_of(first, size):
        top = pl.ds(pl.multiple_of(first, 8 if size % 16 else 16), size)
        bot = pl.ds(pl.multiple_of(first + half, 8 if size % 16 else 16), size)
        return top, bot

    def partial(first, size):
        top, bot = rows_of(first, size)
        both = (
            dot(err_ref[top], q_top, NT) + dot(at_ref[top], gq_top, NT)
            + dot(err_ref[bot], q_bot, NT) + dot(at_ref[bot], gq_bot, NT)
        )
        part_ref[top] = both[:, :wide] + both[:, wide:]

    base, size = 0, half
    bases = []
    first_sem = 0
    for k, (count, digit, peer) in enumerate(phases):
        size = size // count
        land = lands[k]

        def copy(t, base=base, size=size, count=count, digit=digit, peer=peer, land=land, s0=first_sem):
            to = (digit + t) % count
            return pltpu.make_async_remote_copy(
                src_ref=part_ref.at[pl.ds(pl.multiple_of(base + to * size, 8), size)],
                dst_ref=land.at[t],
                send_sem=send_f.at[s0 + t],
                recv_sem=recv_f.at[s0 + t],
                device_id=peer(to),
                device_id_type=MESH,
            )

        if k == 0:
            for t in range(1, count):
                partial((digit + t) % count * size, size)
                if t == 1:
                    pl.semaphore_wait(barrier, n_rep - 1 + across)
                copy(t).start()
            partial(digit * size, size)
            if count == 1:
                pl.semaphore_wait(barrier, n_rep - 1 + across)
        else:
            each(1, count, lambda t: copy(t).start())
        if k == 1:
            for first in range(0, depth, 512):
                last = min(first + 512, depth)
                merged_ref[first:last] = dot(
                    at_ref[first:last], gt_ref[...], NT
                ) + err_ref[first:last].astype(F32)
        each(1, count, lambda t: copy(t).wait())
        base = base + digit * size
        bases.append((base, size, first_sem))
        mine = pl.ds(pl.multiple_of(base, 8), size)
        total = part_ref[mine]
        if count <= 16:
            for t in range(1, count):
                total = total + land[t]
        else:
            total = lax.fori_loop(1, count, lambda t, x: x + land[t], total)
        if k < len(phases) - 1:
            part_ref[mine] = total
        else:
            factor_ref[mine] = total
        first_sem += count

    af, local, halves = [], [], []

    def use(first, size):
        top, bot = rows_of(first, size)
        pair = jnp.concatenate(split(factor_ref[top]), axis=1)
        pair_ref[top] = pair
        pair_t = pair.T
        ft_top = jnp.concatenate([pair_t[:rank], pair_t[wide : wide + rank]], axis=0)
        ft_bot = jnp.concatenate([pair_t[rank:wide], pair_t[wide + rank :]], axis=0)
        af.append(dot(ft_top, at_ref[top]) + dot(ft_bot, at_ref[bot]))
        local.append(dot(ft_top, err_ref[top]) + dot(ft_bot, err_ref[bot]))
        halves.append((pair_t, pair))

    for k in reversed(range(len(phases))):
        count, digit, peer = phases[k]
        base, size, s0 = bases[k]

        def back(t, owner, base=base, size=size, count=count, digit=digit, peer=peer, s0=s0):
            theirs = pl.ds(pl.multiple_of(base - digit * size + owner * size, 8), size)
            return pltpu.make_async_remote_copy(
                src_ref=factor_ref.at[theirs],
                dst_ref=factor_ref.at[theirs],
                send_sem=send_g.at[s0 + t],
                recv_sem=recv_g.at[s0 + t],
                device_id=peer((digit + t) % count),
                device_id_type=MESH,
            )

        each(1, count, lambda t: back(t, digit).start())
        if k == 0:
            use(base, size)
        each(1, count, lambda t: back(t, (digit - t + count) % count).wait_recv())
        if k == 0:
            for t in range(1, count):
                use((digit - t + count) % count * size, size)

    af = sum(af[1:], af[0])
    local = sum(local[1:], local[0])
    af = jnp.concatenate(split(af[:rank] + af[rank:]), axis=0)
    local = local + dot(af, gt_ref[...], NT)
    local = local[:rank] + local[rank:]
    lane_blocks = up(cols, 128) // 128
    for b in range(lane_blocks):
        here = min(128, cols - 128 * b)
        sq_ref[b * rank : (b + 1) * rank, :here] = local[:, 128 * b : 128 * b + here]
        if here < 128:
            sq_ref[b * rank : (b + 1) * rank, here:] = jnp.zeros((rank, 128 - here), F32)
    if sq_ref.shape[0] > lane_blocks * rank:
        sq_ref[lane_blocks * rank :] = jnp.zeros((sq_ref.shape[0] - lane_blocks * rank, 128), F32)

    def scatter(t):
        to = (rep + t) % n_rep
        return pltpu.make_async_remote_copy(
            src_ref=sq_ref.at[pl.ds(pl.multiple_of(to * rows_q, 8), rows_q)],
            dst_ref=lq_ref.at[t],
            send_sem=send_q.at[t],
            recv_sem=recv_q.at[t],
            device_id=(to, shard),
            device_id_type=MESH,
        )

    each(1, n_rep, lambda t: scatter(t).start())

    prod = sum([dot(x, y) for x, y in halves[1:]], dot(*halves[0]))
    g1 = prod[:rank] + prod[wide : wide + rank]
    g2 = prod[rank:wide] + prod[wide + rank :]
    g1 = g1[:, :wide] + g1[:, wide:]
    g2 = g2[:, :wide] + g2[:, wide:]
    gram = g1 + pltpu.roll(g2, rank, 1)
    lane = lax.broadcasted_iota(jnp.int32, (rank, wide), 1)
    row = lax.broadcasted_iota(jnp.int32, (rank, wide), 0)
    aug = jnp.where(lane < rank, gram, jnp.where(lane - rank == row, 1.0, 0.0))
    blocks = [aug[8 * v : 8 * v + 8] for v in range(rank // 8)]
    done = []
    middle = rank // 32
    eliminate(blocks, done, 0, middle)

    for k, (count, digit, peer) in enumerate(phases):
        base, size, s0 = bases[k]

        def sent(t, base=base, size=size, peer=peer, digit=digit, count=count, s0=s0):
            mine = pl.ds(pl.multiple_of(base, 8), size)
            pltpu.make_async_remote_copy(
                src_ref=factor_ref.at[mine],
                dst_ref=factor_ref.at[mine],
                send_sem=send_g.at[s0 + t],
                recv_sem=recv_g.at[s0 + t],
                device_id=peer((digit + t) % count),
                device_id_type=MESH,
            ).wait_send()

        each(1, count, sent)

    each(1, n_rep, lambda t: scatter(t).wait())
    mine_q = pl.ds(pl.multiple_of(rep * rows_q, 8), rows_q)
    total = sq_ref[mine_q]
    if n_rep <= 16:
        for t in range(1, n_rep):
            total = total + lq_ref[t]
    else:
        total = lax.fori_loop(1, n_rep, lambda t, x: x + lq_ref[t], total)
    rq_ref[mine_q] = total / n_rep

    def gather(t, owner):
        theirs = pl.ds(pl.multiple_of(owner * rows_q, 8), rows_q)
        return pltpu.make_async_remote_copy(
            src_ref=rq_ref.at[theirs],
            dst_ref=rq_ref.at[theirs],
            send_sem=send_h.at[t],
            recv_sem=recv_h.at[t],
            device_id=((rep + t) % n_rep, shard),
            device_id_type=MESH,
        )

    each(1, n_rep, lambda t: gather(t, rep).start())

    eliminate(blocks, done, middle, rank // 8)
    inverse = pltpu.roll(jnp.concatenate(done, axis=0), rank, 1)[:, :rank]

    each(1, n_rep, lambda t: gather(t, rep).wait_send())
    each(1, n_rep, lambda t: gather(t, (rep - t + n_rep) % n_rep).wait_recv())

    summed = jnp.concatenate(
        [rq_ref[b * rank : (b + 1) * rank] for b in range(lane_blocks)], axis=1
    )
    right_t = exact(inverse, summed)
    right_ref[...] = right_t[:, :cols]
    mixed_ref[...] = exact(inverse, right_t, TN)[:, :cols]


def finish(pair_ref, merged_ref, mixed_ref, mom_ref, err_new, mom_new, err_ref, new_ref, sem):
    depth, cols = mom_ref.shape
    rank = mixed_ref.shape[0]
    half = pair_ref.shape[0]
    wide = 2 * rank
    m_high, m_low = split(mixed_ref[...])
    gap = jnp.zeros_like(m_high)
    copies = []
    for first, rows, on_high, on_low in (
        (0, min(half, depth), [m_high, gap, m_high, gap], [m_low, gap]),
        (half, max(0, depth - half), [gap, m_high, gap, m_high], [gap, m_low]),
    ):
        on_high = jnp.concatenate(on_high, axis=0)
        on_low = jnp.concatenate(on_low, axis=0)
        for start in range(0, rows, 256):
            size = min(256, rows - start)
            pair = pair_ref[start : start + size]
            approx = dot(pair, on_high) + dot(pair[:, :wide], on_low)
            at = slice(first + start, first + start + size)
            err_ref[at] = (merged_ref[at] - approx).astype(BF16)
            copies.append(pltpu.make_async_copy(err_ref.at[at], err_new.at[at], sem.at[len(copies)]))
            copies[-1].start()
            new_ref[at] = (0.9 * mom_ref[at].astype(F32) + approx).astype(BF16)
            copies.append(pltpu.make_async_copy(new_ref.at[at], mom_new.at[at], sem.at[len(copies)]))
            copies[-1].start()
    for copy in copies:
        copy.wait()


def step(n_rep, n_shard, activations, out_grads, error, momentum, query):
    _, depth, cols = error.shape
    rank = query.shape[1]
    tokens = activations.shape[0]
    half = up(up(-(-depth // 2), 128), 8 * n_rep * n_shard)
    core_n, mid_n, high_n = phases_of(n_rep, n_shard)
    counts = (core_n, mid_n * n_shard, high_n)
    lane_blocks = up(cols, 128) // 128
    rows_q = up(lane_blocks * rank, 8 * n_rep) // n_rep
    sizes, size = [], half
    for count in counts:
        size //= count
        sizes.append(size)
    dma = pltpu.SemaphoreType.DMA
    in_hbm = pl.BlockSpec(memory_space=pltpu.HBM)
    in_vmem = pl.BlockSpec(memory_space=pltpu.VMEM)
    pair, merged, mixed, right = pl.pallas_call(
        functools.partial(kernel, n_rep, n_shard, rows_q),
        out_shape=(
            jax.ShapeDtypeStruct((half, 4 * rank), BF16),
            jax.ShapeDtypeStruct((depth, cols), F32),
            jax.ShapeDtypeStruct((rank, cols), F32),
            jax.ShapeDtypeStruct((rank, cols), F32),
        ),
        in_specs=[in_hbm] * 4,
        out_specs=[in_vmem] * 4,
        scratch_shapes=[
            pltpu.VMEM((2 * half, tokens), BF16),
            pltpu.VMEM((cols, tokens), BF16),
            pltpu.VMEM((2 * half, cols), BF16),
            pltpu.VMEM((rank, cols), F32),
            pltpu.VMEM((half, 2 * rank), F32),
            pltpu.VMEM((half, 2 * rank), F32),
        ]
        + [pltpu.VMEM((c, s, 2 * rank), F32) for c, s in zip(counts, sizes)]
        + [
            pltpu.VMEM((rows_q * n_rep, 128), F32),
            pltpu.VMEM((n_rep, rows_q, 128), F32),
            pltpu.VMEM((rows_q * n_rep, 128), F32),
        ]
        + [dma((5,))]
        + [dma((sum(counts),))] * 4
        + [dma((n_rep,))] * 4,
        compiler_params=pltpu.CompilerParams(
            collective_id=0, has_side_effects=True, vmem_limit_bytes=40 * 1024 * 1024
        ),
    )(*[pltpu.with_memory_space_constraint(x, pltpu.HBM) for x in (activations.T, out_grads.T, error.reshape(depth, cols), query.T)])
    pieces = 2 * (-(-min(half, depth) // 256) + -(-max(0, depth - half) // 256))
    err_new, mom_new = pl.pallas_call(
        finish,
        out_shape=(
            jax.ShapeDtypeStruct((depth, cols), BF16),
            jax.ShapeDtypeStruct((depth, cols), BF16),
        ),
        in_specs=[in_vmem] * 4,
        out_specs=[in_hbm] * 2,
        scratch_shapes=[
            pltpu.VMEM((depth, cols), BF16),
            pltpu.VMEM((depth, cols), BF16),
            dma((pieces,)),
        ],
        compiler_params=pltpu.CompilerParams(vmem_limit_bytes=40 * 1024 * 1024),
    )(pair, merged, mixed, momentum)
    return err_new[None], mom_new, right.T


def solution(mesh):
    return jax.shard_map(
        functools.partial(step, mesh.shape["rep"], mesh.shape["shard"]),
        mesh=mesh,
        in_specs=(
            P("rep", None),
            P("rep", "shard"),
            P("rep", None, "shard"),
            P(None, "shard"),
            P("shard", None),
        ),
        out_specs=(P("rep", None, "shard"), P(None, "shard"), P("shard", None)),
        check_vma=False,
    )
```

```python
import functools

import jax
import jax.numpy as jnp
from jax import lax
from jax.experimental import pallas as pl
from jax.experimental.pallas import tpu as pltpu
from jax.sharding import PartitionSpec as P

MESH = pl.DeviceIdType.MESH
F32 = jnp.float32
BF16 = jnp.bfloat16
NN = (((1,), (0,)), ((), ()))
NT = (((1,), (1,)), ((), ()))
TN = (((0,), (0,)), ((), ()))


def up(value, step):
    return -(-value // step) * step


def dot(a, b, dims=NN):
    return lax.dot_general(a, b, dims, preferred_element_type=F32)


def exact(a, b, dims=NN):
    return lax.dot_general(
        a, b, dims, preferred_element_type=F32, precision=lax.Precision.HIGHEST
    )


def split(x):
    high = x.astype(BF16)
    return high, (x - high.astype(F32)).astype(BF16)


def each(first, last, body):
    if last - first <= 16:
        for t in range(first, last):
            body(t)
    else:
        lax.fori_loop(first, last, lambda t, c: (body(t), c)[1], 0)


def phases_of(n_rep, n_shard):
    core = 2 if n_rep % 2 == 0 else 1
    mid = 2 if n_rep % (2 * core) == 0 else 1
    high = n_rep // (core * mid)
    return core, mid, high


def phases_here(n_rep, n_shard):
    core_n, mid_n, high_n = phases_of(n_rep, n_shard)
    rep = lax.axis_index("rep")
    shard = lax.axis_index("shard")
    core = rep % core_n
    mid = (rep // core_n) % mid_n
    high = rep // (core_n * mid_n)
    low = core_n * mid_n
    return (
        (core_n, core, lambda d: (rep - core + d, shard)),
        (
            mid_n * n_shard,
            mid * n_shard + shard,
            lambda d: (high * low + (d // n_shard) * core_n + core, d % n_shard),
        ),
        (high_n, high, lambda d: (d * low + mid * core_n + core, shard)),
    )


def eliminate(blocks, done, first, last):
    lanes = blocks[0].shape[1]
    sub = lax.broadcasted_iota(jnp.int32, (8, lanes), 0)
    for at in range(first, last):
        held = blocks[at:]
        cols = [
            [jnp.broadcast_to(x[:, 8 * at + k : 8 * at + k + 1], (8, lanes)) for x in held]
            for k in range(8)
        ]
        rows = [jnp.broadcast_to(held[0][k : k + 1], (8, lanes)) for k in range(8)]
        cell = [
            [jnp.broadcast_to(cols[m][0][k : k + 1], (8, lanes)) if m >= k else None for m in range(8)]
            for k in range(8)
        ]
        head = jnp.zeros((8, lanes), F32)
        for k in range(8):
            inv = 1.0 / cell[k][k]
            head = jnp.where(sub == k, rows[k] * lax.rsqrt(cell[k][k]), head)
            for m in range(k + 1, 8):
                ratio = cell[k][m] * inv
                for i in range(k + 1, m + 1):
                    cell[i][m] = cell[i][m] - cell[k][i] * ratio
                rows[m] = rows[m] - rows[k] * ratio
                for v in range(1, len(held)):
                    cols[m][v] = cols[m][v] - cols[k][v] * ratio
            scaled = rows[k] * inv
            for v in range(1, len(held)):
                held[v] = held[v] - cols[k][v] * scaled
        done.append(head)
        blocks[at + 1 :] = held[1:]


def kernel(
    n_rep, n_shard, rows_q, n_slices,
    act_hbm, out_hbm, err_hbm, query_hbm,
    pair_ref, merged_ref, mixed_ref, right_ref,
    at_ref, gt_ref, err_ref, query_ref, part_ref, factor_ref, land0, land1, land2,
    sq_ref, lq_ref, rq_ref,
    in_sem, send_f, recv_f, send_g, recv_g, send_q, recv_q, send_h, recv_h,
):
    depth, cols = err_hbm.shape
    rank = query_ref.shape[0]
    half = part_ref.shape[0]
    wide = 2 * rank
    phases = phases_here(n_rep, n_shard)
    lands = (land0, land1, land2)
    rep = lax.axis_index("rep")
    shard = lax.axis_index("shard")
    core_n, mid_n, high_n = phases_of(n_rep, n_shard)

    cut = up(-(-depth // 2), 16)
    loads = [
        pltpu.make_async_copy(src, dst, in_sem.at[i])
        for i, (src, dst) in enumerate((
            (query_hbm, query_ref),
            (out_hbm, gt_ref),
            (err_hbm.at[:cut], err_ref.at[:cut]),
            (err_hbm.at[cut:], err_ref.at[cut:depth]),
            (act_hbm, at_ref.at[:depth]),
        ))
    ]
    for load in loads:
        load.start()

    barrier = pltpu.get_barrier_semaphore()

    def greet_rep(t):
        pl.semaphore_signal(
            barrier, inc=1, device_id=((rep + t) % n_rep, shard), device_id_type=MESH
        )

    def greet_shard(t):
        _, digit, peer = phases[1]
        mid, other = t // (n_shard - 1), t % (n_shard - 1)
        to = mid * n_shard + (shard + 1 + other) % n_shard
        pl.semaphore_signal(barrier, inc=1, device_id=peer(to), device_id_type=MESH)

    each(1, n_rep, greet_rep)
    across = mid_n * (n_shard - 1)
    if across:
        each(0, across, greet_shard)

    if 2 * half > depth:
        err_ref[depth:] = jnp.zeros((2 * half - depth, cols), BF16)
        at_ref[depth:] = jnp.zeros((2 * half - depth, at_ref.shape[1]), BF16)

    loads[0].wait()
    loads[1].wait()
    query = query_ref[...]
    none = jnp.zeros_like(query)
    q_top = jnp.concatenate(split(jnp.concatenate([query, none], axis=0)), axis=0)
    q_bot = jnp.concatenate(split(jnp.concatenate([none, query], axis=0)), axis=0)

    def through(q):
        gq = dot(q, gt_ref[...])
        return jnp.concatenate(split(gq[:wide] + gq[wide:]), axis=0)

    gq_top, gq_bot = through(q_top), through(q_bot)
    for load in loads[2:]:
        load.wait()

    def rows_of(first, size):
        top = pl.ds(pl.multiple_of(first, 8 if size % 16 else 16), size)
        bot = pl.ds(pl.multiple_of(first + half, 8 if size % 16 else 16), size)
        return top, bot

    def partial(first, size):
        top, bot = rows_of(first, size)
        both = (
            dot(err_ref[top], q_top, NT) + dot(at_ref[top], gq_top, NT)
            + dot(err_ref[bot], q_bot, NT) + dot(at_ref[bot], gq_bot, NT)
        )
        part_ref[top] = both[:, :wide] + both[:, wide:]

    n_phases = len(phases)
    sems, per_slice = [], 0
    for count, _, _ in phases:
        sems.append(per_slice)
        per_slice += count
    slices = range(n_slices)
    spans = []
    for s in slices:
        base, size = s * (half // n_slices), half // n_slices
        spans.append([])
        for count, digit, _ in phases:
            size = size // count
            spans[s].append((base, size))
            base = base + digit * size

    def rows_at(s, k, owner):
        base, size = spans[s][k]
        return pl.ds(pl.multiple_of(base + owner * size, 8), size)

    def forth(s, k, t):
        count, digit, peer = phases[k]
        to = (digit + t) % count
        at = s * per_slice + sems[k] + t
        return pltpu.make_async_remote_copy(
            src_ref=part_ref.at[rows_at(s, k, to)],
            dst_ref=lands[k].at[s * count + t],
            send_sem=send_f.at[at],
            recv_sem=recv_f.at[at],
            device_id=peer(to),
            device_id_type=MESH,
        )

    def back(s, k, t, owner):
        count, digit, peer = phases[k]
        at = s * per_slice + sems[k] + t
        return pltpu.make_async_remote_copy(
            src_ref=factor_ref.at[rows_at(s, k, owner)],
            dst_ref=factor_ref.at[rows_at(s, k, owner)],
            send_sem=send_g.at[at],
            recv_sem=recv_g.at[at],
            device_id=peer((digit + t) % count),
            device_id_type=MESH,
        )

    def send_forth(s, k):
        each(1, phases[k][0], lambda t: forth(s, k, t).start())

    def add_up(s, k):
        count, digit, _ = phases[k]
        each(1, count, lambda t: forth(s, k, t).wait())
        mine = rows_at(s, k, digit)
        total = part_ref[mine]
        land = lands[k]
        if count <= 16:
            for t in range(1, count):
                total = total + land[s * count + t]
        else:
            total = lax.fori_loop(1, count, lambda t, x: x + land[s * count + t], total)
        if k < n_phases - 1:
            part_ref[mine] = total
        else:
            factor_ref[mine] = total

    def send_back(s, k):
        each(1, phases[k][0], lambda t: back(s, k, t, phases[k][1]).start())

    def arrive(s, k):
        count, digit, _ = phases[k]
        each(1, count, lambda t: back(s, k, t, (digit - t + count) % count).wait_recv())

    count, digit, _ = phases[0]
    for s in slices:
        base, size = spans[s][0]
        for t in range(1, count):
            partial(base + (digit + t) % count * size, size)
        if s == 0:
            pl.semaphore_wait(barrier, n_rep - 1 + across)
        send_forth(s, 0)
    for s in slices:
        base, size = spans[s][0]
        partial(base + digit * size, size)
    for k in range(1, n_phases):
        for s in slices:
            add_up(s, k - 1)
            send_forth(s, k)
        if k == 1:
            for first in range(0, depth, 512):
                last = min(first + 512, depth)
                merged_ref[first:last] = dot(
                    at_ref[first:last], gt_ref[...], NT
                ) + err_ref[first:last].astype(F32)
    for s in slices:
        add_up(s, n_phases - 1)
        send_back(s, n_phases - 1)

    af, local, halves = [], [], []

    def use(first, size):
        top, bot = rows_of(first, size)
        pair = jnp.concatenate(split(factor_ref[top]), axis=1)
        pair_ref[top] = pair
        pair_t = pair.T
        ft_top = jnp.concatenate([pair_t[:rank], pair_t[wide : wide + rank]], axis=0)
        ft_bot = jnp.concatenate([pair_t[rank:wide], pair_t[wide + rank :]], axis=0)
        af.append(dot(ft_top, at_ref[top]) + dot(ft_bot, at_ref[bot]))
        local.append(dot(ft_top, err_ref[top]) + dot(ft_bot, err_ref[bot]))
        halves.append((pair_t, pair))

    for k in range(n_phases - 1, 0, -1):
        for s in slices:
            arrive(s, k)
            send_back(s, k - 1)
            if k == 1:
                base, size = spans[s][0]
                use(base + digit * size, size)
    for s in slices:
        arrive(s, 0)
        base, size = spans[s][0]
        for t in range(1, count):
            use(base + (digit - t + count) % count * size, size)

    af = sum(af[1:], af[0])
    local = sum(local[1:], local[0])
    af = jnp.concatenate(split(af[:rank] + af[rank:]), axis=0)
    local = local + dot(af, gt_ref[...], NT)
    local = local[:rank] + local[rank:]
    lane_blocks = up(cols, 128) // 128
    for b in range(lane_blocks):
        here = min(128, cols - 128 * b)
        sq_ref[b * rank : (b + 1) * rank, :here] = local[:, 128 * b : 128 * b + here]
        if here < 128:
            sq_ref[b * rank : (b + 1) * rank, here:] = jnp.zeros((rank, 128 - here), F32)
    if sq_ref.shape[0] > lane_blocks * rank:
        sq_ref[lane_blocks * rank :] = jnp.zeros((sq_ref.shape[0] - lane_blocks * rank, 128), F32)

    def scatter(t):
        to = (rep + t) % n_rep
        return pltpu.make_async_remote_copy(
            src_ref=sq_ref.at[pl.ds(pl.multiple_of(to * rows_q, 8), rows_q)],
            dst_ref=lq_ref.at[t],
            send_sem=send_q.at[t],
            recv_sem=recv_q.at[t],
            device_id=(to, shard),
            device_id_type=MESH,
        )

    each(1, n_rep, lambda t: scatter(t).start())

    prod = sum([dot(x, y) for x, y in halves[1:]], dot(*halves[0]))
    g1 = prod[:rank] + prod[wide : wide + rank]
    g2 = prod[rank:wide] + prod[wide + rank :]
    g1 = g1[:, :wide] + g1[:, wide:]
    g2 = g2[:, :wide] + g2[:, wide:]
    gram = g1 + pltpu.roll(g2, rank, 1)
    lane = lax.broadcasted_iota(jnp.int32, (rank, wide), 1)
    row = lax.broadcasted_iota(jnp.int32, (rank, wide), 0)
    aug = jnp.where(lane < rank, gram, jnp.where(lane - rank == row, 1.0, 0.0))
    blocks = [aug[8 * v : 8 * v + 8] for v in range(rank // 8)]
    done = []
    middle = rank // 32
    eliminate(blocks, done, 0, middle)

    for s in slices:
        for k in range(n_phases):
            each(1, phases[k][0], lambda t: back(s, k, t, phases[k][1]).wait_send())

    each(1, n_rep, lambda t: scatter(t).wait())
    mine_q = pl.ds(pl.multiple_of(rep * rows_q, 8), rows_q)
    total = sq_ref[mine_q]
    if n_rep <= 16:
        for t in range(1, n_rep):
            total = total + lq_ref[t]
    else:
        total = lax.fori_loop(1, n_rep, lambda t, x: x + lq_ref[t], total)
    rq_ref[mine_q] = total / n_rep

    def gather(t, owner):
        theirs = pl.ds(pl.multiple_of(owner * rows_q, 8), rows_q)
        return pltpu.make_async_remote_copy(
            src_ref=rq_ref.at[theirs],
            dst_ref=rq_ref.at[theirs],
            send_sem=send_h.at[t],
            recv_sem=recv_h.at[t],
            device_id=((rep + t) % n_rep, shard),
            device_id_type=MESH,
        )

    each(1, n_rep, lambda t: gather(t, rep).start())

    eliminate(blocks, done, middle, rank // 8)
    inverse = pltpu.roll(jnp.concatenate(done, axis=0), rank, 1)[:, :rank]

    each(1, n_rep, lambda t: gather(t, rep).wait_send())
    each(1, n_rep, lambda t: gather(t, (rep - t + n_rep) % n_rep).wait_recv())

    summed = jnp.concatenate(
        [rq_ref[b * rank : (b + 1) * rank] for b in range(lane_blocks)], axis=1
    )
    right_t = exact(inverse, summed)
    right_ref[...] = right_t[:, :cols]
    mixed_ref[...] = exact(inverse, right_t, TN)[:, :cols]


def finish(
    pair_ref, merged_ref, mixed_ref, mom_ref, right_ref,
    err_new, mom_new, query_new,
    err_ref, new_ref, sem,
):
    depth, cols = mom_ref.shape
    rank = mixed_ref.shape[0]
    half = pair_ref.shape[0]
    wide = 2 * rank
    m_high, m_low = split(mixed_ref[...])
    gap = jnp.zeros_like(m_high)
    copies = [pltpu.make_async_copy(right_ref, query_new, sem.at[0])]
    copies[0].start()
    for first, rows, on_high, on_low in (
        (0, min(half, depth), [m_high, gap, m_high, gap], [m_low, gap]),
        (half, max(0, depth - half), [gap, m_high, gap, m_high], [gap, m_low]),
    ):
        on_high = jnp.concatenate(on_high, axis=0)
        on_low = jnp.concatenate(on_low, axis=0)
        for start in range(0, rows, 256):
            size = min(256, rows - start)
            pair = pair_ref[start : start + size]
            approx = dot(pair, on_high) + dot(pair[:, :wide], on_low)
            at = slice(first + start, first + start + size)
            err_ref[at] = (merged_ref[at] - approx).astype(BF16)
            copies.append(pltpu.make_async_copy(err_ref.at[at], err_new.at[at], sem.at[len(copies)]))
            copies[-1].start()
            new_ref[at] = (0.9 * mom_ref[at].astype(F32) + approx).astype(BF16)
            copies.append(pltpu.make_async_copy(new_ref.at[at], mom_new.at[at], sem.at[len(copies)]))
            copies[-1].start()
    for copy in copies:
        copy.wait()


def step(n_rep, n_shard, activations, out_grads, error, momentum, query):
    _, depth, cols = error.shape
    rank = query.shape[1]
    tokens = activations.shape[0]
    half = up(up(-(-depth // 2), 128), 8 * n_rep * n_shard)
    core_n, mid_n, high_n = phases_of(n_rep, n_shard)
    counts = (core_n, mid_n * n_shard, high_n)
    lane_blocks = up(cols, 128) // 128
    rows_q = up(lane_blocks * rank, 8 * n_rep) // n_rep
    n_slices = 2 if half // (8 * n_rep * n_shard) % 2 == 0 else 1
    sizes, size = [], half // n_slices
    for count in counts:
        size //= count
        sizes.append(size)
    dma = pltpu.SemaphoreType.DMA
    in_hbm = pl.BlockSpec(memory_space=pltpu.HBM)
    in_vmem = pl.BlockSpec(memory_space=pltpu.VMEM)
    pair, merged, mixed, right = pl.pallas_call(
        functools.partial(kernel, n_rep, n_shard, rows_q, n_slices),
        out_shape=(
            jax.ShapeDtypeStruct((half, 4 * rank), BF16),
            jax.ShapeDtypeStruct((depth, cols), F32),
            jax.ShapeDtypeStruct((rank, cols), F32),
            jax.ShapeDtypeStruct((rank, cols), F32),
        ),
        in_specs=[in_hbm] * 4,
        out_specs=[in_vmem] * 4,
        scratch_shapes=[
            pltpu.VMEM((2 * half, tokens), BF16),
            pltpu.VMEM((cols, tokens), BF16),
            pltpu.VMEM((2 * half, cols), BF16),
            pltpu.VMEM((rank, cols), F32),
            pltpu.VMEM((half, 2 * rank), F32),
            pltpu.VMEM((half, 2 * rank), F32),
        ]
        + [pltpu.VMEM((n_slices * c, s, 2 * rank), F32) for c, s in zip(counts, sizes)]
        + [
            pltpu.VMEM((rows_q * n_rep, 128), F32),
            pltpu.VMEM((n_rep, rows_q, 128), F32),
            pltpu.VMEM((rows_q * n_rep, 128), F32),
        ]
        + [dma((5,))]
        + [dma((n_slices * sum(counts),))] * 4
        + [dma((n_rep,))] * 4,
        compiler_params=pltpu.CompilerParams(
            collective_id=0, has_side_effects=True, vmem_limit_bytes=40 * 1024 * 1024
        ),
    )(*[pltpu.with_memory_space_constraint(x, pltpu.HBM) for x in (activations.T, out_grads.T, error.reshape(depth, cols), query.T)])
    pieces = 2 * (-(-min(half, depth) // 256) + -(-max(0, depth - half) // 256))
    err_new, mom_new, right = pl.pallas_call(
        finish,
        out_shape=(
            jax.ShapeDtypeStruct((depth, cols), BF16),
            jax.ShapeDtypeStruct((depth, cols), BF16),
            jax.ShapeDtypeStruct((rank, cols), F32),
        ),
        in_specs=[in_vmem] * 5,
        out_specs=[in_hbm] * 3,
        scratch_shapes=[
            pltpu.VMEM((depth, cols), BF16),
            pltpu.VMEM((depth, cols), BF16),
            dma((pieces + 1,)),
        ],
        compiler_params=pltpu.CompilerParams(vmem_limit_bytes=40 * 1024 * 1024),
    )(pair, merged, mixed, momentum, right)
    return err_new[None], mom_new, right.T


def solution(mesh):
    return jax.shard_map(
        functools.partial(step, mesh.shape["rep"], mesh.shape["shard"]),
        mesh=mesh,
        in_specs=(
            P("rep", None),
            P("rep", "shard"),
            P("rep", None, "shard"),
            P(None, "shard"),
            P("shard", None),
        ),
        out_specs=(P("rep", None, "shard"), P(None, "shard"), P("shard", None)),
        check_vma=False,
    )
```

```python
import functools

import jax
import jax.numpy as jnp
from jax import lax
from jax.experimental import pallas as pl
from jax.experimental.pallas import tpu as pltpu
from jax.sharding import PartitionSpec as P

MESH = pl.DeviceIdType.MESH
F32 = jnp.float32
BF16 = jnp.bfloat16
NN = (((1,), (0,)), ((), ()))
NT = (((1,), (1,)), ((), ()))
TN = (((0,), (0,)), ((), ()))


def up(value, step):
    return -(-value // step) * step


def dot(a, b, dims=NN):
    return lax.dot_general(a, b, dims, preferred_element_type=F32)


def exact(a, b, dims=NN):
    return lax.dot_general(
        a, b, dims, preferred_element_type=F32, precision=lax.Precision.HIGHEST
    )


def split(x):
    high = x.astype(BF16)
    return high, (x - high.astype(F32)).astype(BF16)


def each(first, last, body):
    if last - first <= 16:
        for t in range(first, last):
            body(t)
    else:
        lax.fori_loop(first, last, lambda t, c: (body(t), c)[1], 0)


def rem(a, b):
    return lax.rem(a, jnp.int32(b))


def div(a, b):
    return lax.div(a, jnp.int32(b))


def phases_of(n_rep, n_shard):
    core = 2 if n_rep % 2 == 0 else 1
    mid = 2 if n_rep % (2 * core) == 0 else 1
    high = n_rep // (core * mid)
    return core, mid, high


def phases_here(n_rep, n_shard):
    core_n, mid_n, high_n = phases_of(n_rep, n_shard)
    rep = lax.axis_index("rep")
    shard = lax.axis_index("shard")
    core = rem(rep, core_n)
    mid = rem(div(rep, core_n), mid_n)
    high = div(rep, core_n * mid_n)
    low = core_n * mid_n
    return (
        (core_n, core, lambda d: (rep - core + d, shard)),
        (
            mid_n * n_shard,
            mid * n_shard + shard,
            lambda d: (high * low + div(d, n_shard) * core_n + core, rem(d, n_shard)),
        ),
        (high_n, high, lambda d: (d * low + mid * core_n + core, shard)),
    )


def eliminate(blocks, done, first, last):
    lanes = blocks[0].shape[1]
    sub = lax.broadcasted_iota(jnp.int32, (8, lanes), 0)
    for at in range(first, last):
        held = blocks[at:]
        cols = [
            [jnp.broadcast_to(x[:, 8 * at + k : 8 * at + k + 1], (8, lanes)) for x in held]
            for k in range(8)
        ]
        rows = [jnp.broadcast_to(held[0][k : k + 1], (8, lanes)) for k in range(8)]
        cell = [
            [jnp.broadcast_to(cols[m][0][k : k + 1], (8, lanes)) if m >= k else None for m in range(8)]
            for k in range(8)
        ]
        head = jnp.zeros((8, lanes), F32)
        for k in range(8):
            inv = 1.0 / cell[k][k]
            head = jnp.where(sub == k, rows[k] * lax.rsqrt(cell[k][k]), head)
            for m in range(k + 1, 8):
                ratio = cell[k][m] * inv
                for i in range(k + 1, m + 1):
                    cell[i][m] = cell[i][m] - cell[k][i] * ratio
                rows[m] = rows[m] - rows[k] * ratio
                for v in range(1, len(held)):
                    cols[m][v] = cols[m][v] - cols[k][v] * ratio
            scaled = rows[k] * inv
            for v in range(1, len(held)):
                held[v] = held[v] - cols[k][v] * scaled
        done.append(head)
        blocks[at + 1 :] = held[1:]


def kernel(
    n_rep, n_shard, rows_q, n_slices,
    act_hbm, out_hbm, err_hbm, query_hbm, mom_hbm,
    pair_ref, merged_ref, mixed_ref, right_ref, mom_ref,
    at_ref, gt_ref, err_ref, query_ref, part_ref, factor_ref, land0, land1, land2,
    sq_ref, lq_ref, zq_ref, rq_ref,
    in_sem, send_f, recv_f, send_g, recv_g, send_q, recv_q, send_z, recv_z, send_h, recv_h,
):
    depth, cols = err_hbm.shape
    rank = query_ref.shape[0]
    half = part_ref.shape[0]
    wide = 2 * rank
    phases = phases_here(n_rep, n_shard)
    lands = (land0, land1, land2)
    rep = lax.axis_index("rep")
    shard = lax.axis_index("shard")
    core_n, mid_n, high_n = phases_of(n_rep, n_shard)

    pieces = [(query_hbm, query_ref), (out_hbm, gt_ref)]
    part = half // n_slices
    for s in range(n_slices):
        for first in (s * part, half + s * part):
            last = min(first + part, depth)
            if first < last:
                pieces.append((err_hbm.at[first:last], err_ref.at[first:last]))
                pieces.append((act_hbm.at[first:last], at_ref.at[first:last]))
    loads = [pltpu.make_async_copy(a, b, in_sem.at[i]) for i, (a, b) in enumerate(pieces)]
    for load in loads:
        load.start()
    mom_load = pltpu.make_async_copy(mom_hbm, mom_ref, in_sem.at[len(pieces)])
    waiting = loads[2:]

    barrier = pltpu.get_barrier_semaphore()

    low_n = core_n * mid_n
    low = rem(rep, low_n)
    around = low_n * n_shard

    def greet_near(t):
        to = rem(low * n_shard + shard + t, around)
        to = (rep - low + div(to, n_shard), rem(to, n_shard))
        pl.semaphore_signal(barrier, inc=1, device_id=to, device_id_type=MESH)

    def greet_far(t):
        to = phases[2][2](rem(phases[2][1] + t, high_n))
        pl.semaphore_signal(barrier, inc=1, device_id=to, device_id_type=MESH)

    each(1, around, greet_near)
    each(1, high_n, greet_far)

    if 2 * half > depth:
        err_ref[depth:] = jnp.zeros((2 * half - depth, cols), BF16)
        at_ref[depth:] = jnp.zeros((2 * half - depth, at_ref.shape[1]), BF16)

    loads[0].wait()
    loads[1].wait()
    query = query_ref[...]
    none = jnp.zeros_like(query)
    q_top = jnp.concatenate(split(jnp.concatenate([query, none], axis=0)), axis=0)
    q_bot = jnp.concatenate(split(jnp.concatenate([none, query], axis=0)), axis=0)

    def through(q):
        gq = dot(q, gt_ref[...])
        return jnp.concatenate(split(gq[:wide] + gq[wide:]), axis=0)

    gq_top, gq_bot = through(q_top), through(q_bot)
    def rows_of(first, size):
        top = pl.ds(pl.multiple_of(first, 8 if size % 16 else 16), size)
        bot = pl.ds(pl.multiple_of(first + half, 8 if size % 16 else 16), size)
        return top, bot

    def partial(first, size):
        top, bot = rows_of(first, size)
        both = (
            dot(err_ref[top], q_top, NT) + dot(at_ref[top], gq_top, NT)
            + dot(err_ref[bot], q_bot, NT) + dot(at_ref[bot], gq_bot, NT)
        )
        part_ref[top] = both[:, :wide] + both[:, wide:]

    n_phases = len(phases)
    sems, per_slice = [], 0
    for count, _, _ in phases:
        sems.append(per_slice)
        per_slice += count
    slices = range(n_slices)
    spans = []
    for s in slices:
        base, size = s * (half // n_slices), half // n_slices
        spans.append([])
        for count, digit, _ in phases:
            size = size // count
            spans[s].append((base, size))
            base = base + digit * size

    def rows_at(s, k, owner):
        base, size = spans[s][k]
        return pl.ds(pl.multiple_of(base + owner * size, 8), size)

    def forth(s, k, t):
        count, digit, peer = phases[k]
        to = rem(digit + t, count)
        at = s * per_slice + sems[k] + t
        return pltpu.make_async_remote_copy(
            src_ref=part_ref.at[rows_at(s, k, to)],
            dst_ref=lands[k].at[s * count + t],
            send_sem=send_f.at[at],
            recv_sem=recv_f.at[at],
            device_id=peer(to),
            device_id_type=MESH,
        )

    def back(s, k, t, owner):
        count, digit, peer = phases[k]
        at = s * per_slice + sems[k] + t
        return pltpu.make_async_remote_copy(
            src_ref=factor_ref.at[rows_at(s, k, owner)],
            dst_ref=factor_ref.at[rows_at(s, k, owner)],
            send_sem=send_g.at[at],
            recv_sem=recv_g.at[at],
            device_id=peer(rem(digit + t, count)),
            device_id_type=MESH,
        )

    def send_forth(s, k):
        each(1, phases[k][0], lambda t: forth(s, k, t).start())

    def add_up(s, k):
        count, digit, _ = phases[k]
        each(1, count, lambda t: forth(s, k, t).wait())
        mine = rows_at(s, k, digit)
        total = part_ref[mine]
        land = lands[k]
        if count <= 16:
            for t in range(1, count):
                total = total + land[s * count + t]
        else:
            total = lax.fori_loop(1, count, lambda t, x: x + land[s * count + t], total)
        if k < n_phases - 1:
            part_ref[mine] = total
        else:
            factor_ref[mine] = total

    def send_back(s, k):
        each(1, phases[k][0], lambda t: back(s, k, t, phases[k][1]).start())

    def arrive(s, k):
        count, digit, _ = phases[k]
        each(1, count, lambda t: back(s, k, t, rem(digit - t + count, count)).wait_recv())

    count, digit, _ = phases[0]
    for s in slices:
        base, size = spans[s][0]
        for load in waiting[4 * s : 4 * s + 4] if s < n_slices - 1 else waiting[4 * s :]:
            load.wait()
        for t in range(1, count):
            partial(base + rem(digit + t, count) * size, size)
        if s == 0:
            pl.semaphore_wait(barrier, around - 1 + high_n - 1)
        send_forth(s, 0)
    for s in slices:
        base, size = spans[s][0]
        partial(base + digit * size, size)
    mom_load.start()
    for k in range(1, n_phases):
        for s in slices:
            add_up(s, k - 1)
            send_forth(s, k)
        if k == 1:
            for first in range(0, depth, 512):
                last = min(first + 512, depth)
                merged_ref[first:last] = dot(
                    at_ref[first:last], gt_ref[...], NT
                ) + err_ref[first:last].astype(F32)
    for s in slices:
        add_up(s, n_phases - 1)
        send_back(s, n_phases - 1)

    af, local, halves = [], [], []

    def use(first, size):
        top, bot = rows_of(first, size)
        pair = jnp.concatenate(split(factor_ref[top]), axis=1)
        pair_ref[top] = pair
        pair_t = pair.T
        ft_top = jnp.concatenate([pair_t[:rank], pair_t[wide : wide + rank]], axis=0)
        ft_bot = jnp.concatenate([pair_t[rank:wide], pair_t[wide + rank :]], axis=0)
        af.append(dot(ft_top, at_ref[top]) + dot(ft_bot, at_ref[bot]))
        local.append(dot(ft_top, err_ref[top]) + dot(ft_bot, err_ref[bot]))
        halves.append((pair_t, pair))

    for k in range(n_phases - 1, 0, -1):
        for s in slices:
            arrive(s, k)
            send_back(s, k - 1)
            if k == 1:
                base, size = spans[s][0]
                use(base + digit * size, size)
    for s in slices:
        arrive(s, 0)
        base, size = spans[s][0]
        for t in range(1, count):
            use(base + rem(digit - t + count, count) * size, size)

    af = sum(af[1:], af[0])
    local = sum(local[1:], local[0])
    af = jnp.concatenate(split(af[:rank] + af[rank:]), axis=0)
    local = local + dot(af, gt_ref[...], NT)
    local = local[:rank] + local[rank:]
    lane_blocks = up(cols, 128) // 128
    for b in range(lane_blocks):
        here = min(128, cols - 128 * b)
        sq_ref[b * rank : (b + 1) * rank, :here] = local[:, 128 * b : 128 * b + here]
        if here < 128:
            sq_ref[b * rank : (b + 1) * rank, here:] = jnp.zeros((rank, 128 - here), F32)
    if sq_ref.shape[0] > lane_blocks * rank:
        sq_ref[lane_blocks * rank :] = jnp.zeros((sq_ref.shape[0] - lane_blocks * rank, 128), F32)

    def scatter(t):
        to = rem(low + t, low_n)
        return pltpu.make_async_remote_copy(
            src_ref=sq_ref.at[pl.ds(pl.multiple_of(to * rows_q, 8), rows_q)],
            dst_ref=lq_ref.at[t],
            send_sem=send_q.at[t],
            recv_sem=recv_q.at[t],
            device_id=(rep - low + to, shard),
            device_id_type=MESH,
        )

    each(1, low_n, lambda t: scatter(t).start())

    prod = sum([dot(x, y) for x, y in halves[1:]], dot(*halves[0]))
    g1 = prod[:rank] + prod[wide : wide + rank]
    g2 = prod[rank:wide] + prod[wide + rank :]
    g1 = g1[:, :wide] + g1[:, wide:]
    g2 = g2[:, :wide] + g2[:, wide:]
    gram = g1 + pltpu.roll(g2, rank, 1)
    lane = lax.broadcasted_iota(jnp.int32, (rank, wide), 1)
    row = lax.broadcasted_iota(jnp.int32, (rank, wide), 0)
    aug = jnp.where(lane < rank, gram, jnp.where(lane - rank == row, 1.0, 0.0))
    blocks = [aug[8 * v : 8 * v + 8] for v in range(rank // 8)]
    done = []
    middle = rank // 8 * 5 // 8

    each(1, low_n, lambda t: scatter(t).wait())
    mine_q = pl.ds(pl.multiple_of(low * rows_q, 8), rows_q)
    total = sq_ref[mine_q]
    for t in range(1, low_n):
        total = total + lq_ref[t]
    high = phases[2][1]
    zq_ref[high] = total

    def spread(t, owner):
        return pltpu.make_async_remote_copy(
            src_ref=zq_ref.at[owner],
            dst_ref=zq_ref.at[owner],
            send_sem=send_z.at[t],
            recv_sem=recv_z.at[t],
            device_id=phases[2][2](rem(high + t, high_n)),
            device_id_type=MESH,
        )

    each(1, high_n, lambda t: spread(t, high).start())
    eliminate(blocks, done, 0, middle)
    for s in slices:
        for k in range(n_phases):
            each(1, phases[k][0], lambda t: back(s, k, t, phases[k][1]).wait_send())

    each(1, high_n, lambda t: spread(t, high).wait_send())
    each(1, high_n, lambda t: spread(t, rem(high - t + high_n, high_n)).wait_recv())
    total = zq_ref[0]
    if high_n <= 16:
        for t in range(1, high_n):
            total = total + zq_ref[t]
    else:
        total = lax.fori_loop(1, high_n, lambda t, x: x + zq_ref[t], total)
    rq_ref[mine_q] = total / n_rep

    def gather(t, owner):
        theirs = pl.ds(pl.multiple_of(owner * rows_q, 8), rows_q)
        return pltpu.make_async_remote_copy(
            src_ref=rq_ref.at[theirs],
            dst_ref=rq_ref.at[theirs],
            send_sem=send_h.at[t],
            recv_sem=recv_h.at[t],
            device_id=(rep - low + rem(low + t, low_n), shard),
            device_id_type=MESH,
        )

    each(1, low_n, lambda t: gather(t, low).start())

    eliminate(blocks, done, middle, rank // 8)
    inverse = pltpu.roll(jnp.concatenate(done, axis=0), rank, 1)[:, :rank]

    mom_load.wait()
    each(1, low_n, lambda t: gather(t, low).wait_send())
    each(1, low_n, lambda t: gather(t, rem(low - t + low_n, low_n)).wait_recv())

    summed = jnp.concatenate(
        [rq_ref[b * rank : (b + 1) * rank] for b in range(lane_blocks)], axis=1
    )
    right_t = exact(inverse, summed)
    right_ref[...] = right_t[:, :cols]
    mixed_ref[...] = exact(inverse, right_t, TN)[:, :cols]


def finish(
    pair_ref, merged_ref, mixed_ref, mom_ref, right_ref,
    err_new, mom_new, query_new,
    err_ref, new_ref, sem,
):
    depth, cols = mom_ref.shape
    rank = mixed_ref.shape[0]
    half = pair_ref.shape[0]
    wide = 2 * rank
    m_high, m_low = split(mixed_ref[...])
    gap = jnp.zeros_like(m_high)
    copies = [pltpu.make_async_copy(right_ref, query_new, sem.at[0])]
    copies[0].start()
    for first, rows, on_high, on_low in (
        (0, min(half, depth), [m_high, gap, m_high, gap], [m_low, gap]),
        (half, max(0, depth - half), [gap, m_high, gap, m_high], [gap, m_low]),
    ):
        on_high = jnp.concatenate(on_high, axis=0)
        on_low = jnp.concatenate(on_low, axis=0)
        for start in range(0, rows, 256):
            size = min(256, rows - start)
            pair = pair_ref[start : start + size]
            approx = dot(pair, on_high) + dot(pair[:, :wide], on_low)
            at = slice(first + start, first + start + size)
            err_ref[at] = (merged_ref[at] - approx).astype(BF16)
            copies.append(pltpu.make_async_copy(err_ref.at[at], err_new.at[at], sem.at[len(copies)]))
            copies[-1].start()
            new_ref[at] = (0.9 * mom_ref[at].astype(F32) + approx).astype(BF16)
            copies.append(pltpu.make_async_copy(new_ref.at[at], mom_new.at[at], sem.at[len(copies)]))
            copies[-1].start()
    for copy in copies:
        copy.wait()


def step(n_rep, n_shard, activations, out_grads, error, momentum, query):
    _, depth, cols = error.shape
    rank = query.shape[1]
    tokens = activations.shape[0]
    half = up(up(-(-depth // 2), 128), 8 * n_rep * n_shard)
    core_n, mid_n, high_n = phases_of(n_rep, n_shard)
    counts = (core_n, mid_n * n_shard, high_n)
    lane_blocks = up(cols, 128) // 128
    low_n = core_n * mid_n
    rows_q = up(lane_blocks * rank, 8 * low_n) // low_n
    n_slices = 2 if half // (8 * n_rep * n_shard) % 2 == 0 else 1
    sizes, size = [], half // n_slices
    for count in counts:
        size //= count
        sizes.append(size)
    dma = pltpu.SemaphoreType.DMA
    in_hbm = pl.BlockSpec(memory_space=pltpu.HBM)
    in_vmem = pl.BlockSpec(memory_space=pltpu.VMEM)
    pair, merged, mixed, right, mom = pl.pallas_call(
        functools.partial(kernel, n_rep, n_shard, rows_q, n_slices),
        out_shape=(
            jax.ShapeDtypeStruct((half, 4 * rank), BF16),
            jax.ShapeDtypeStruct((depth, cols), F32),
            jax.ShapeDtypeStruct((rank, cols), F32),
            jax.ShapeDtypeStruct((rank, cols), F32),
            jax.ShapeDtypeStruct((depth, cols), BF16),
        ),
        in_specs=[in_hbm] * 5,
        out_specs=[in_vmem] * 5,
        scratch_shapes=[
            pltpu.VMEM((2 * half, tokens), BF16),
            pltpu.VMEM((cols, tokens), BF16),
            pltpu.VMEM((2 * half, cols), BF16),
            pltpu.VMEM((rank, cols), F32),
            pltpu.VMEM((half, 2 * rank), F32),
            pltpu.VMEM((half, 2 * rank), F32),
        ]
        + [pltpu.VMEM((n_slices * c, s, 2 * rank), F32) for c, s in zip(counts, sizes)]
        + [
            pltpu.VMEM((rows_q * low_n, 128), F32),
            pltpu.VMEM((low_n, rows_q, 128), F32),
            pltpu.VMEM((high_n, rows_q, 128), F32),
            pltpu.VMEM((rows_q * low_n, 128), F32),
        ]
        + [dma((4 * n_slices + 3,))]
        + [dma((n_slices * sum(counts),))] * 4
        + [dma((low_n,))] * 2
        + [dma((high_n,))] * 2
        + [dma((low_n,))] * 2,
        compiler_params=pltpu.CompilerParams(
            collective_id=0, has_side_effects=True, vmem_limit_bytes=40 * 1024 * 1024
        ),
    )(*[pltpu.with_memory_space_constraint(x, pltpu.HBM) for x in (activations.T, out_grads.T, error.reshape(depth, cols), query.T, momentum)])
    pieces = 2 * (-(-min(half, depth) // 256) + -(-max(0, depth - half) // 256))
    err_new, mom_new, right = pl.pallas_call(
        finish,
        out_shape=(
            jax.ShapeDtypeStruct((depth, cols), BF16),
            jax.ShapeDtypeStruct((depth, cols), BF16),
            jax.ShapeDtypeStruct((rank, cols), F32),
        ),
        in_specs=[in_vmem] * 5,
        out_specs=[in_hbm] * 3,
        scratch_shapes=[
            pltpu.VMEM((depth, cols), BF16),
            pltpu.VMEM((depth, cols), BF16),
            dma((pieces + 1,)),
        ],
        compiler_params=pltpu.CompilerParams(vmem_limit_bytes=40 * 1024 * 1024),
    )(pair, merged, mixed, mom, right)
    return err_new[None], mom_new, right.T


def solution(mesh):
    return jax.shard_map(
        functools.partial(step, mesh.shape["rep"], mesh.shape["shard"]),
        mesh=mesh,
        in_specs=(
            P("rep", None),
            P("rep", "shard"),
            P("rep", None, "shard"),
            P(None, "shard"),
            P("shard", None),
        ),
        out_specs=(P("rep", None, "shard"), P(None, "shard"), P("shard", None)),
        check_vma=False,
    )
```

```python
import functools

import jax
import jax.numpy as jnp
from jax import lax
from jax.experimental import pallas as pl
from jax.experimental.pallas import tpu as pltpu
from jax.sharding import PartitionSpec as P

MESH = pl.DeviceIdType.MESH
F32 = jnp.float32
BF16 = jnp.bfloat16
NN = (((1,), (0,)), ((), ()))
NT = (((1,), (1,)), ((), ()))
TN = (((0,), (0,)), ((), ()))


def up(value, step):
    return -(-value // step) * step


def dot(a, b, dims=NN):
    return lax.dot_general(a, b, dims, preferred_element_type=F32)


def exact(a, b, dims=NN):
    return lax.dot_general(
        a, b, dims, preferred_element_type=F32, precision=lax.Precision.HIGHEST
    )


def split(x):
    high = x.astype(BF16)
    return high, (x - high.astype(F32)).astype(BF16)


def each(first, last, body):
    if last - first <= 16:
        for t in range(first, last):
            body(t)
    else:
        lax.fori_loop(first, last, lambda t, c: (body(t), c)[1], 0)


def rem(a, b):
    return lax.rem(a, jnp.int32(b))


def div(a, b):
    return lax.div(a, jnp.int32(b))


def phases_of(n_rep, n_shard):
    core = 2 if n_rep % 2 == 0 else 1
    mid = 2 if n_rep % (2 * core) == 0 else 1
    high = n_rep // (core * mid)
    return core, mid, high


def near_of(high_n):
    return 2 if high_n % 2 == 0 else 1


def phases_here(n_rep, n_shard):
    core_n, mid_n, high_n = phases_of(n_rep, n_shard)
    near_n = near_of(high_n)
    rep = lax.axis_index("rep")
    shard = lax.axis_index("shard")
    core = rem(rep, core_n)
    mid = rem(div(rep, core_n), mid_n)
    high = div(rep, core_n * mid_n)
    low = core_n * mid_n
    return (
        (core_n, core, lambda d: (rep - core + d, shard)),
        (
            mid_n * n_shard,
            mid * n_shard + shard,
            lambda d: (high * low + div(d, n_shard) * core_n + core, rem(d, n_shard)),
        ),
        (
            near_n,
            rem(high, near_n),
            lambda d: ((high - rem(high, near_n) + d) * low + mid * core_n + core, shard),
        ),
    ), (high_n, high, lambda d: (d * low + mid * core_n + core, shard)), (
        high_n // near_n,
        div(high, near_n),
        lambda d: ((d * near_n + rem(high, near_n)) * low + mid * core_n + core, shard),
    )


def eliminate(blocks, done, first, last):
    lanes = blocks[0].shape[1]
    sub = lax.broadcasted_iota(jnp.int32, (8, lanes), 0)
    for at in range(first, last):
        held = blocks[at:]
        cols = [
            [jnp.broadcast_to(x[:, 8 * at + k : 8 * at + k + 1], (8, lanes)) for x in held]
            for k in range(8)
        ]
        rows = [jnp.broadcast_to(held[0][k : k + 1], (8, lanes)) for k in range(8)]
        cell = [
            [jnp.broadcast_to(cols[m][0][k : k + 1], (8, lanes)) if m >= k else None for m in range(8)]
            for k in range(8)
        ]
        head = jnp.zeros((8, lanes), F32)
        for k in range(8):
            inv = 1.0 / cell[k][k]
            head = jnp.where(sub == k, rows[k] * lax.rsqrt(cell[k][k]), head)
            for m in range(k + 1, 8):
                ratio = cell[k][m] * inv
                for i in range(k + 1, m + 1):
                    cell[i][m] = cell[i][m] - cell[k][i] * ratio
                rows[m] = rows[m] - rows[k] * ratio
                for v in range(1, len(held)):
                    cols[m][v] = cols[m][v] - cols[k][v] * ratio
            scaled = rows[k] * inv
            for v in range(1, len(held)):
                held[v] = held[v] - cols[k][v] * scaled
        done.append(head)
        blocks[at + 1 :] = held[1:]


def kernel(
    n_rep, n_shard, rows_q, n_slices,
    act_hbm, out_hbm, err_hbm, query_hbm, mom_hbm,
    pair_ref, merged_ref, mixed_ref, right_ref, mom_ref,
    at_ref, gt_ref, err_ref, query_ref, part_ref, factor_ref, land0, land1, land2, ex_ref,
    sq_ref, lq_ref, zq_ref, rq_ref,
    in_sem, send_f, recv_f, send_g, recv_g, send_q, recv_q, send_z, recv_z, send_h, recv_h, send_x, recv_x,
):
    depth, cols = err_hbm.shape
    rank = query_ref.shape[0]
    half = part_ref.shape[0]
    wide = 2 * rank
    phases, far, cross = phases_here(n_rep, n_shard)
    lands = (land0, land1, land2)
    rep = lax.axis_index("rep")
    shard = lax.axis_index("shard")
    core_n, mid_n, high_n = phases_of(n_rep, n_shard)

    pieces = [(query_hbm, query_ref), (out_hbm, gt_ref)]
    part = half // n_slices
    for s in range(n_slices):
        for first in (s * part, half + s * part):
            last = min(first + part, depth)
            if first < last:
                pieces.append((err_hbm.at[first:last], err_ref.at[first:last]))
                pieces.append((act_hbm.at[first:last], at_ref.at[first:last]))
    loads = [pltpu.make_async_copy(a, b, in_sem.at[i]) for i, (a, b) in enumerate(pieces)]
    for load in loads:
        load.start()
    mom_load = pltpu.make_async_copy(mom_hbm, mom_ref, in_sem.at[len(pieces)])
    waiting = loads[2:]

    barrier = pltpu.get_barrier_semaphore()

    low_n = core_n * mid_n
    low = rem(rep, low_n)
    around = low_n * n_shard

    def greet_near(t):
        to = rem(low * n_shard + shard + t, around)
        to = (rep - low + div(to, n_shard), rem(to, n_shard))
        pl.semaphore_signal(barrier, inc=1, device_id=to, device_id_type=MESH)

    def greet_far(t):
        to = far[2](rem(far[1] + t, high_n))
        pl.semaphore_signal(barrier, inc=1, device_id=to, device_id_type=MESH)

    each(1, around, greet_near)
    each(1, high_n, greet_far)

    if 2 * half > depth:
        err_ref[depth:] = jnp.zeros((2 * half - depth, cols), BF16)
        at_ref[depth:] = jnp.zeros((2 * half - depth, at_ref.shape[1]), BF16)

    loads[0].wait()
    loads[1].wait()
    query = query_ref[...]
    none = jnp.zeros_like(query)
    q_top = jnp.concatenate(split(jnp.concatenate([query, none], axis=0)), axis=0)
    q_bot = jnp.concatenate(split(jnp.concatenate([none, query], axis=0)), axis=0)

    def through(q):
        gq = dot(q, gt_ref[...])
        return jnp.concatenate(split(gq[:wide] + gq[wide:]), axis=0)

    gq_top, gq_bot = through(q_top), through(q_bot)
    def rows_of(first, size):
        top = pl.ds(pl.multiple_of(first, 8 if size % 16 else 16), size)
        bot = pl.ds(pl.multiple_of(first + half, 8 if size % 16 else 16), size)
        return top, bot

    def partial(first, size):
        top, bot = rows_of(first, size)
        both = (
            dot(err_ref[top], q_top, NT) + dot(at_ref[top], gq_top, NT)
            + dot(err_ref[bot], q_bot, NT) + dot(at_ref[bot], gq_bot, NT)
        )
        part_ref[top] = both[:, :wide] + both[:, wide:]

    n_phases = len(phases)
    sems, per_slice = [], 0
    for count, _, _ in phases:
        sems.append(per_slice)
        per_slice += count
    slices = range(n_slices)
    spans = []
    for s in slices:
        base, size = s * (half // n_slices), half // n_slices
        spans.append([])
        for count, digit, _ in phases:
            size = size // count
            spans[s].append((base, size))
            base = base + digit * size

    def rows_at(s, k, owner):
        base, size = spans[s][k]
        return pl.ds(pl.multiple_of(base + owner * size, 8), size)

    def forth(s, k, t):
        count, digit, peer = phases[k]
        to = rem(digit + t, count)
        at = s * per_slice + sems[k] + t
        return pltpu.make_async_remote_copy(
            src_ref=part_ref.at[rows_at(s, k, to)],
            dst_ref=lands[k].at[s * count + t],
            send_sem=send_f.at[at],
            recv_sem=recv_f.at[at],
            device_id=peer(to),
            device_id_type=MESH,
        )

    def back(s, k, t, owner):
        count, digit, peer = phases[k]
        at = s * per_slice + sems[k] + t
        return pltpu.make_async_remote_copy(
            src_ref=factor_ref.at[rows_at(s, k, owner)],
            dst_ref=factor_ref.at[rows_at(s, k, owner)],
            send_sem=send_g.at[at],
            recv_sem=recv_g.at[at],
            device_id=peer(rem(digit + t, count)),
            device_id_type=MESH,
        )

    def send_forth(s, k):
        each(1, phases[k][0], lambda t: forth(s, k, t).start())

    def add_up(s, k):
        count, digit, _ = phases[k]
        each(1, count, lambda t: forth(s, k, t).wait())
        mine = rows_at(s, k, digit)
        total = part_ref[mine]
        land = lands[k]
        if count <= 16:
            for t in range(1, count):
                total = total + land[s * count + t]
        else:
            total = lax.fori_loop(1, count, lambda t, x: x + land[s * count + t], total)
        if k < n_phases - 1:
            part_ref[mine] = total
        else:
            ex_ref[s * cross[0] + cross[1]] = total

    def swap(s, t, owner):
        count, digit, peer = cross
        return pltpu.make_async_remote_copy(
            src_ref=ex_ref.at[s * count + owner],
            dst_ref=ex_ref.at[s * count + owner],
            send_sem=send_x.at[s * count + t],
            recv_sem=recv_x.at[s * count + t],
            device_id=peer(rem(digit + t, count)),
            device_id_type=MESH,
        )

    def send_back(s, k):
        each(1, phases[k][0], lambda t: back(s, k, t, phases[k][1]).start())

    def arrive(s, k):
        count, digit, _ = phases[k]
        each(1, count, lambda t: back(s, k, t, rem(digit - t + count, count)).wait_recv())

    count, digit, _ = phases[0]
    for s in slices:
        base, size = spans[s][0]
        for load in waiting[4 * s : 4 * s + 4] if s < n_slices - 1 else waiting[4 * s :]:
            load.wait()
        for t in range(1, count):
            partial(base + rem(digit + t, count) * size, size)
        if s == 0:
            pl.semaphore_wait(barrier, around - 1 + high_n - 1)
        send_forth(s, 0)
    for s in slices:
        base, size = spans[s][0]
        partial(base + digit * size, size)
    mom_load.start()
    for k in range(1, n_phases):
        for s in slices:
            add_up(s, k - 1)
            send_forth(s, k)
        if k == 1:
            for first in range(0, depth, 512):
                last = min(first + 512, depth)
                merged_ref[first:last] = dot(
                    at_ref[first:last], gt_ref[...], NT
                ) + err_ref[first:last].astype(F32)
    for s in slices:
        add_up(s, n_phases - 1)
        each(1, cross[0], lambda t: swap(s, t, cross[1]).start())
    for s in slices:
        n, digit, _ = cross
        each(1, n, lambda t: swap(s, t, rem(digit - t + n, n)).wait_recv())
        total = ex_ref[s * n]
        if n <= 16:
            for t in range(1, n):
                total = total + ex_ref[s * n + t]
        else:
            total = lax.fori_loop(1, n, lambda t, x: x + ex_ref[s * n + t], total)
        factor_ref[rows_at(s, n_phases - 1, phases[-1][1])] = total
        send_back(s, n_phases - 1)
    count, digit, _ = phases[0]

    af, local, halves = [], [], []

    def use(first, size):
        top, bot = rows_of(first, size)
        pair = jnp.concatenate(split(factor_ref[top]), axis=1)
        pair_ref[top] = pair
        pair_t = pair.T
        ft_top = jnp.concatenate([pair_t[:rank], pair_t[wide : wide + rank]], axis=0)
        ft_bot = jnp.concatenate([pair_t[rank:wide], pair_t[wide + rank :]], axis=0)
        af.append(dot(ft_top, at_ref[top]) + dot(ft_bot, at_ref[bot]))
        local.append(dot(ft_top, err_ref[top]) + dot(ft_bot, err_ref[bot]))
        halves.append((pair_t, pair))

    for k in range(n_phases - 1, 0, -1):
        for s in slices:
            arrive(s, k)
            send_back(s, k - 1)
            if k == 1:
                base, size = spans[s][0]
                use(base + digit * size, size)
    for s in slices:
        arrive(s, 0)
        base, size = spans[s][0]
        for t in range(1, count):
            use(base + rem(digit - t + count, count) * size, size)

    af = sum(af[1:], af[0])
    local = sum(local[1:], local[0])
    af = jnp.concatenate(split(af[:rank] + af[rank:]), axis=0)
    local = local + dot(af, gt_ref[...], NT)
    local = local[:rank] + local[rank:]
    lane_blocks = up(cols, 128) // 128
    for b in range(lane_blocks):
        here = min(128, cols - 128 * b)
        sq_ref[b * rank : (b + 1) * rank, :here] = local[:, 128 * b : 128 * b + here]
        if here < 128:
            sq_ref[b * rank : (b + 1) * rank, here:] = jnp.zeros((rank, 128 - here), F32)
    if sq_ref.shape[0] > lane_blocks * rank:
        sq_ref[lane_blocks * rank :] = jnp.zeros((sq_ref.shape[0] - lane_blocks * rank, 128), F32)

    def scatter(t):
        to = rem(low + t, low_n)
        return pltpu.make_async_remote_copy(
            src_ref=sq_ref.at[pl.ds(pl.multiple_of(to * rows_q, 8), rows_q)],
            dst_ref=lq_ref.at[t],
            send_sem=send_q.at[t],
            recv_sem=recv_q.at[t],
            device_id=(rep - low + to, shard),
            device_id_type=MESH,
        )

    each(1, low_n, lambda t: scatter(t).start())

    prod = sum([dot(x, y) for x, y in halves[1:]], dot(*halves[0]))
    g1 = prod[:rank] + prod[wide : wide + rank]
    g2 = prod[rank:wide] + prod[wide + rank :]
    g1 = g1[:, :wide] + g1[:, wide:]
    g2 = g2[:, :wide] + g2[:, wide:]
    gram = g1 + pltpu.roll(g2, rank, 1)
    lane = lax.broadcasted_iota(jnp.int32, (rank, wide), 1)
    row = lax.broadcasted_iota(jnp.int32, (rank, wide), 0)
    aug = jnp.where(lane < rank, gram, jnp.where(lane - rank == row, 1.0, 0.0))
    blocks = [aug[8 * v : 8 * v + 8] for v in range(rank // 8)]
    done = []
    middle = rank // 8 * 5 // 8

    each(1, low_n, lambda t: scatter(t).wait())
    mine_q = pl.ds(pl.multiple_of(low * rows_q, 8), rows_q)
    total = sq_ref[mine_q]
    for t in range(1, low_n):
        total = total + lq_ref[t]
    high = far[1]
    zq_ref[high] = total

    def spread(t, owner):
        return pltpu.make_async_remote_copy(
            src_ref=zq_ref.at[owner],
            dst_ref=zq_ref.at[owner],
            send_sem=send_z.at[t],
            recv_sem=recv_z.at[t],
            device_id=far[2](rem(high + t, high_n)),
            device_id_type=MESH,
        )

    each(1, high_n, lambda t: spread(t, high).start())
    eliminate(blocks, done, 0, middle)
    for s in slices:
        for k in range(n_phases):
            each(1, phases[k][0], lambda t: back(s, k, t, phases[k][1]).wait_send())
        each(1, cross[0], lambda t: swap(s, t, cross[1]).wait_send())

    each(1, high_n, lambda t: spread(t, high).wait_send())
    each(1, high_n, lambda t: spread(t, rem(high - t + high_n, high_n)).wait_recv())
    total = zq_ref[0]
    if high_n <= 16:
        for t in range(1, high_n):
            total = total + zq_ref[t]
    else:
        total = lax.fori_loop(1, high_n, lambda t, x: x + zq_ref[t], total)
    rq_ref[mine_q] = total / n_rep

    def gather(t, owner):
        theirs = pl.ds(pl.multiple_of(owner * rows_q, 8), rows_q)
        return pltpu.make_async_remote_copy(
            src_ref=rq_ref.at[theirs],
            dst_ref=rq_ref.at[theirs],
            send_sem=send_h.at[t],
            recv_sem=recv_h.at[t],
            device_id=(rep - low + rem(low + t, low_n), shard),
            device_id_type=MESH,
        )

    each(1, low_n, lambda t: gather(t, low).start())

    eliminate(blocks, done, middle, rank // 8)
    inverse = pltpu.roll(jnp.concatenate(done, axis=0), rank, 1)[:, :rank]
    both = jnp.concatenate([inverse, exact(inverse, inverse, TN)], axis=0)

    mom_load.wait()
    each(1, low_n, lambda t: gather(t, low).wait_send())
    each(1, low_n, lambda t: gather(t, rem(low - t + low_n, low_n)).wait_recv())

    summed = jnp.concatenate(
        [rq_ref[b * rank : (b + 1) * rank] for b in range(lane_blocks)], axis=1
    )
    both = exact(both, summed)
    right_ref[...] = both[:rank, :cols]
    mixed_ref[...] = both[rank:, :cols]


def finish(
    pair_ref, merged_ref, mixed_ref, mom_ref, right_ref,
    err_new, mom_new, query_new,
    err_ref, new_ref, sem,
):
    depth, cols = mom_ref.shape
    rank = mixed_ref.shape[0]
    half = pair_ref.shape[0]
    wide = 2 * rank
    m_high, m_low = split(mixed_ref[...])
    gap = jnp.zeros_like(m_high)
    copies = [pltpu.make_async_copy(right_ref, query_new, sem.at[0])]
    copies[0].start()
    for first, rows, on_high, on_low in (
        (0, min(half, depth), [m_high, gap, m_high, gap], [m_low, gap]),
        (half, max(0, depth - half), [gap, m_high, gap, m_high], [gap, m_low]),
    ):
        on_high = jnp.concatenate(on_high, axis=0)
        on_low = jnp.concatenate(on_low, axis=0)
        for start in range(0, rows, 256):
            size = min(256, rows - start)
            pair = pair_ref[start : start + size]
            approx = dot(pair, on_high) + dot(pair[:, :wide], on_low)
            at = slice(first + start, first + start + size)
            err_ref[at] = (merged_ref[at] - approx).astype(BF16)
            copies.append(pltpu.make_async_copy(err_ref.at[at], err_new.at[at], sem.at[len(copies)]))
            copies[-1].start()
            new_ref[at] = (0.9 * mom_ref[at].astype(F32) + approx).astype(BF16)
            copies.append(pltpu.make_async_copy(new_ref.at[at], mom_new.at[at], sem.at[len(copies)]))
            copies[-1].start()
    for copy in copies:
        copy.wait()


def step(n_rep, n_shard, activations, out_grads, error, momentum, query):
    _, depth, cols = error.shape
    rank = query.shape[1]
    tokens = activations.shape[0]
    half = up(up(-(-depth // 2), 128), 8 * n_rep * n_shard)
    core_n, mid_n, high_n = phases_of(n_rep, n_shard)
    near_n = near_of(high_n)
    counts = (core_n, mid_n * n_shard, near_n)
    n_cross = high_n // near_n
    lane_blocks = up(cols, 128) // 128
    low_n = core_n * mid_n
    rows_q = up(lane_blocks * rank, 8 * low_n) // low_n
    n_slices = 2 if half // (8 * n_rep * n_shard) % 2 == 0 else 1
    sizes, size = [], half // n_slices
    for count in counts:
        size //= count
        sizes.append(size)
    dma = pltpu.SemaphoreType.DMA
    in_hbm = pl.BlockSpec(memory_space=pltpu.HBM)
    in_vmem = pl.BlockSpec(memory_space=pltpu.VMEM)
    pair, merged, mixed, right, mom = pl.pallas_call(
        functools.partial(kernel, n_rep, n_shard, rows_q, n_slices),
        out_shape=(
            jax.ShapeDtypeStruct((half, 4 * rank), BF16),
            jax.ShapeDtypeStruct((depth, cols), F32),
            jax.ShapeDtypeStruct((rank, cols), F32),
            jax.ShapeDtypeStruct((rank, cols), F32),
            jax.ShapeDtypeStruct((depth, cols), BF16),
        ),
        in_specs=[in_hbm] * 5,
        out_specs=[in_vmem] * 5,
        scratch_shapes=[
            pltpu.VMEM((2 * half, tokens), BF16),
            pltpu.VMEM((cols, tokens), BF16),
            pltpu.VMEM((2 * half, cols), BF16),
            pltpu.VMEM((rank, cols), F32),
            pltpu.VMEM((half, 2 * rank), F32),
            pltpu.VMEM((half, 2 * rank), F32),
        ]
        + [pltpu.VMEM((n_slices * c, s, 2 * rank), F32) for c, s in zip(counts, sizes)]
        + [
            pltpu.VMEM((n_slices * n_cross, sizes[-1], 2 * rank), F32),
            pltpu.VMEM((rows_q * low_n, 128), F32),
            pltpu.VMEM((low_n, rows_q, 128), F32),
            pltpu.VMEM((high_n, rows_q, 128), F32),
            pltpu.VMEM((rows_q * low_n, 128), F32),
        ]
        + [dma((4 * n_slices + 3,))]
        + [dma((n_slices * sum(counts),))] * 4
        + [dma((low_n,))] * 2
        + [dma((high_n,))] * 2
        + [dma((low_n,))] * 2
        + [dma((n_slices * n_cross,))] * 2,
        compiler_params=pltpu.CompilerParams(
            collective_id=0, has_side_effects=True, vmem_limit_bytes=40 * 1024 * 1024
        ),
    )(*[pltpu.with_memory_space_constraint(x, pltpu.HBM) for x in (activations.T, out_grads.T, error.reshape(depth, cols), query.T, momentum)])
    pieces = 2 * (-(-min(half, depth) // 256) + -(-max(0, depth - half) // 256))
    err_new, mom_new, right = pl.pallas_call(
        finish,
        out_shape=(
            jax.ShapeDtypeStruct((depth, cols), BF16),
            jax.ShapeDtypeStruct((depth, cols), BF16),
            jax.ShapeDtypeStruct((rank, cols), F32),
        ),
        in_specs=[in_vmem] * 5,
        out_specs=[in_hbm] * 3,
        scratch_shapes=[
            pltpu.VMEM((depth, cols), BF16),
            pltpu.VMEM((depth, cols), BF16),
            dma((pieces + 1,)),
        ],
        compiler_params=pltpu.CompilerParams(vmem_limit_bytes=40 * 1024 * 1024),
    )(pair, merged, mixed, mom, right)
    return err_new[None], mom_new, right.T


def solution(mesh):
    return jax.shard_map(
        functools.partial(step, mesh.shape["rep"], mesh.shape["shard"]),
        mesh=mesh,
        in_specs=(
            P("rep", None),
            P("rep", "shard"),
            P("rep", None, "shard"),
            P(None, "shard"),
            P("shard", None),
        ),
        out_specs=(P("rep", None, "shard"), P(None, "shard"), P("shard", None)),
        check_vma=False,
    )
```

```python
import functools

import jax
import jax.numpy as jnp
from jax import lax
from jax.experimental import pallas as pl
from jax.experimental.pallas import tpu as pltpu
from jax.sharding import PartitionSpec as P

MESH = pl.DeviceIdType.MESH
F32 = jnp.float32
BF16 = jnp.bfloat16
NN = (((1,), (0,)), ((), ()))
NT = (((1,), (1,)), ((), ()))
TN = (((0,), (0,)), ((), ()))


def up(value, step):
    return -(-value // step) * step


def dot(a, b, dims=NN):
    return lax.dot_general(a, b, dims, preferred_element_type=F32)


def exact(a, b, dims=NN):
    return lax.dot_general(
        a, b, dims, preferred_element_type=F32, precision=lax.Precision.HIGHEST
    )


def split(x):
    high = x.astype(BF16)
    return high, (x - high.astype(F32)).astype(BF16)


def each(first, last, body):
    if last - first <= 16:
        for t in range(first, last):
            body(t)
    else:
        lax.fori_loop(first, last, lambda t, c: (body(t), c)[1], 0)


def rem(a, b):
    return lax.rem(a, jnp.int32(b))


def div(a, b):
    return lax.div(a, jnp.int32(b))


def phases_of(n_rep, n_shard):
    core = 2 if n_rep % 2 == 0 else 1
    mid = 2 if n_rep % (2 * core) == 0 else 1
    high = n_rep // (core * mid)
    return core, mid, high


def phases_here(n_rep, n_shard):
    core_n, mid_n, high_n = phases_of(n_rep, n_shard)
    rep = lax.axis_index("rep")
    shard = lax.axis_index("shard")
    high = div(rep, core_n * mid_n)
    low = core_n * mid_n
    place = rem(rep, low) * n_shard + shard
    return (
        (
            low * n_shard,
            place,
            lambda d: (high * low + div(d, n_shard), rem(d, n_shard)),
        ),
        (high_n, high, lambda d: (d * low + rem(rep, low), shard)),
    )


def eliminate(blocks, done, first, last):
    lanes = blocks[0].shape[1]
    sub = lax.broadcasted_iota(jnp.int32, (8, lanes), 0)
    for at in range(first, last):
        held = blocks[at:]
        cols = [
            [jnp.broadcast_to(x[:, 8 * at + k : 8 * at + k + 1], (8, lanes)) for x in held]
            for k in range(8)
        ]
        rows = [jnp.broadcast_to(held[0][k : k + 1], (8, lanes)) for k in range(8)]
        cell = [
            [jnp.broadcast_to(cols[m][0][k : k + 1], (8, lanes)) if m >= k else None for m in range(8)]
            for k in range(8)
        ]
        head = jnp.zeros((8, lanes), F32)
        for k in range(8):
            inv = 1.0 / cell[k][k]
            head = jnp.where(sub == k, rows[k] * lax.rsqrt(cell[k][k]), head)
            for m in range(k + 1, 8):
                ratio = cell[k][m] * inv
                for i in range(k + 1, m + 1):
                    cell[i][m] = cell[i][m] - cell[k][i] * ratio
                rows[m] = rows[m] - rows[k] * ratio
                for v in range(1, len(held)):
                    cols[m][v] = cols[m][v] - cols[k][v] * ratio
            scaled = rows[k] * inv
            for v in range(1, len(held)):
                held[v] = held[v] - cols[k][v] * scaled
        done.append(head)
        blocks[at + 1 :] = held[1:]


def kernel(
    n_rep, n_shard, rows_q, n_slices,
    act_hbm, out_hbm, err_hbm, query_hbm, mom_hbm,
    pair_ref, merged_ref, mixed_ref, right_ref, mom_ref,
    at_ref, gt_ref, err_ref, query_ref, part_ref, factor_ref, land0, land1,
    sq_ref, lq_ref, zq_ref, rq_ref,
    in_sem, send_f, recv_f, send_g, recv_g, send_q, recv_q, send_z, recv_z, send_h, recv_h,
):
    depth, cols = err_hbm.shape
    rank = query_ref.shape[0]
    half = part_ref.shape[0]
    wide = 2 * rank
    phases = phases_here(n_rep, n_shard)
    lands = (land0, land1)
    rep = lax.axis_index("rep")
    shard = lax.axis_index("shard")
    core_n, mid_n, high_n = phases_of(n_rep, n_shard)

    pieces = [(query_hbm, query_ref), (out_hbm, gt_ref)]
    part = half // n_slices
    for s in range(n_slices):
        for first in (s * part, half + s * part):
            last = min(first + part, depth)
            if first < last:
                pieces.append((err_hbm.at[first:last], err_ref.at[first:last]))
                pieces.append((act_hbm.at[first:last], at_ref.at[first:last]))
    loads = [pltpu.make_async_copy(a, b, in_sem.at[i]) for i, (a, b) in enumerate(pieces)]
    for load in loads:
        load.start()
    mom_load = pltpu.make_async_copy(mom_hbm, mom_ref, in_sem.at[len(pieces)])
    waiting = loads[2:]

    barrier = pltpu.get_barrier_semaphore()

    low_n = core_n * mid_n
    low = rem(rep, low_n)
    around = low_n * n_shard

    def greet_near(t):
        to = rem(low * n_shard + shard + t, around)
        to = (rep - low + div(to, n_shard), rem(to, n_shard))
        pl.semaphore_signal(barrier, inc=1, device_id=to, device_id_type=MESH)

    def greet_far(t):
        to = phases[1][2](rem(phases[1][1] + t, high_n))
        pl.semaphore_signal(barrier, inc=1, device_id=to, device_id_type=MESH)

    each(1, around, greet_near)
    each(1, high_n, greet_far)

    if 2 * half > depth:
        err_ref[depth:] = jnp.zeros((2 * half - depth, cols), BF16)
        at_ref[depth:] = jnp.zeros((2 * half - depth, at_ref.shape[1]), BF16)

    loads[0].wait()
    loads[1].wait()
    query = query_ref[...]
    none = jnp.zeros_like(query)
    q_top = jnp.concatenate(split(jnp.concatenate([query, none], axis=0)), axis=0)
    q_bot = jnp.concatenate(split(jnp.concatenate([none, query], axis=0)), axis=0)

    def through(q):
        gq = dot(q, gt_ref[...])
        return jnp.concatenate(split(gq[:wide] + gq[wide:]), axis=0)

    gq_top, gq_bot = through(q_top), through(q_bot)
    def rows_of(first, size):
        top = pl.ds(pl.multiple_of(first, 8 if size % 16 else 16), size)
        bot = pl.ds(pl.multiple_of(first + half, 8 if size % 16 else 16), size)
        return top, bot

    def partial(first, size):
        top, bot = rows_of(first, size)
        both = (
            dot(err_ref[top], q_top, NT) + dot(at_ref[top], gq_top, NT)
            + dot(err_ref[bot], q_bot, NT) + dot(at_ref[bot], gq_bot, NT)
        )
        part_ref[top] = both[:, :wide] + both[:, wide:]

    n_phases = len(phases)
    sems, per_slice = [], 0
    for count, _, _ in phases:
        sems.append(per_slice)
        per_slice += count
    slices = range(n_slices)
    spans = []
    for s in slices:
        base, size = s * (half // n_slices), half // n_slices
        spans.append([])
        for count, digit, _ in phases:
            size = size // count
            spans[s].append((base, size))
            base = base + digit * size

    def rows_at(s, k, owner):
        base, size = spans[s][k]
        return pl.ds(pl.multiple_of(base + owner * size, 8), size)

    def forth(s, k, t):
        count, digit, peer = phases[k]
        to = rem(digit + t, count)
        at = s * per_slice + sems[k] + t
        return pltpu.make_async_remote_copy(
            src_ref=part_ref.at[rows_at(s, k, to)],
            dst_ref=lands[k].at[s * count + t],
            send_sem=send_f.at[at],
            recv_sem=recv_f.at[at],
            device_id=peer(to),
            device_id_type=MESH,
        )

    def back(s, k, t, owner):
        count, digit, peer = phases[k]
        at = s * per_slice + sems[k] + t
        return pltpu.make_async_remote_copy(
            src_ref=factor_ref.at[rows_at(s, k, owner)],
            dst_ref=factor_ref.at[rows_at(s, k, owner)],
            send_sem=send_g.at[at],
            recv_sem=recv_g.at[at],
            device_id=peer(rem(digit + t, count)),
            device_id_type=MESH,
        )

    def send_forth(s, k):
        each(1, phases[k][0], lambda t: forth(s, k, t).start())

    def add_up(s, k):
        count, digit, _ = phases[k]
        each(1, count, lambda t: forth(s, k, t).wait())
        mine = rows_at(s, k, digit)
        total = part_ref[mine]
        land = lands[k]
        if count <= 16:
            for t in range(1, count):
                total = total + land[s * count + t]
        else:
            total = lax.fori_loop(1, count, lambda t, x: x + land[s * count + t], total)
        if k < n_phases - 1:
            part_ref[mine] = total
        else:
            factor_ref[mine] = total

    def send_back(s, k):
        each(1, phases[k][0], lambda t: back(s, k, t, phases[k][1]).start())

    def arrive(s, k):
        count, digit, _ = phases[k]
        each(1, count, lambda t: back(s, k, t, rem(digit - t + count, count)).wait_recv())

    count, digit, _ = phases[0]
    for s in slices:
        base, size = spans[s][0]
        for load in waiting[4 * s : 4 * s + 4] if s < n_slices - 1 else waiting[4 * s :]:
            load.wait()
        for t in range(1, count):
            partial(base + rem(digit + t, count) * size, size)
            if s == 0 and t == 1:
                pl.semaphore_wait(barrier, around - 1 + high_n - 1)
            forth(s, 0, t).start()
    for s in slices:
        base, size = spans[s][0]
        partial(base + digit * size, size)
    mom_load.start()
    for first in range(0, depth, 512):
        last = min(first + 512, depth)
        merged_ref[first:last] = dot(
            at_ref[first:last], gt_ref[...], NT
        ) + err_ref[first:last].astype(F32)
    for k in range(1, n_phases):
        for s in slices:
            add_up(s, k - 1)
            send_forth(s, k)
    for s in slices:
        add_up(s, n_phases - 1)
        send_back(s, n_phases - 1)

    af, local, halves = [], [], []

    def use(first, size):
        top, bot = rows_of(first, size)
        pair = jnp.concatenate(split(factor_ref[top]), axis=1)
        pair_ref[top] = pair
        pair_t = pair.T
        ft_top = jnp.concatenate([pair_t[:rank], pair_t[wide : wide + rank]], axis=0)
        ft_bot = jnp.concatenate([pair_t[rank:wide], pair_t[wide + rank :]], axis=0)
        af.append(dot(ft_top, at_ref[top]) + dot(ft_bot, at_ref[bot]))
        local.append(dot(ft_top, err_ref[top]) + dot(ft_bot, err_ref[bot]))
        halves.append((pair_t, pair))

    for k in range(n_phases - 1, 0, -1):
        for s in slices:
            arrive(s, k)
            send_back(s, k - 1)
            if k == 1:
                base, size = spans[s][0]
                use(base + digit * size, size)
    for s in slices:
        base, size = spans[s][0]
        for t in range(1, count):
            back(s, 0, t, rem(digit - t + count, count)).wait_recv()
            use(base + rem(digit - t + count, count) * size, size)

    af = sum(af[1:], af[0])
    local = sum(local[1:], local[0])
    af = jnp.concatenate(split(af[:rank] + af[rank:]), axis=0)
    local = local + dot(af, gt_ref[...], NT)
    local = local[:rank] + local[rank:]
    lane_blocks = up(cols, 128) // 128
    for b in range(lane_blocks):
        here = min(128, cols - 128 * b)
        sq_ref[b * rank : (b + 1) * rank, :here] = local[:, 128 * b : 128 * b + here]
        if here < 128:
            sq_ref[b * rank : (b + 1) * rank, here:] = jnp.zeros((rank, 128 - here), F32)
    if sq_ref.shape[0] > lane_blocks * rank:
        sq_ref[lane_blocks * rank :] = jnp.zeros((sq_ref.shape[0] - lane_blocks * rank, 128), F32)

    def scatter(t):
        to = rem(low + t, low_n)
        return pltpu.make_async_remote_copy(
            src_ref=sq_ref.at[pl.ds(pl.multiple_of(to * rows_q, 8), rows_q)],
            dst_ref=lq_ref.at[t],
            send_sem=send_q.at[t],
            recv_sem=recv_q.at[t],
            device_id=(rep - low + to, shard),
            device_id_type=MESH,
        )

    each(1, low_n, lambda t: scatter(t).start())

    prod = sum([dot(x, y) for x, y in halves[1:]], dot(*halves[0]))
    g1 = prod[:rank] + prod[wide : wide + rank]
    g2 = prod[rank:wide] + prod[wide + rank :]
    g1 = g1[:, :wide] + g1[:, wide:]
    g2 = g2[:, :wide] + g2[:, wide:]
    gram = g1 + pltpu.roll(g2, rank, 1)
    lane = lax.broadcasted_iota(jnp.int32, (rank, wide), 1)
    row = lax.broadcasted_iota(jnp.int32, (rank, wide), 0)
    aug = jnp.where(lane < rank, gram, jnp.where(lane - rank == row, 1.0, 0.0))
    blocks = [aug[8 * v : 8 * v + 8] for v in range(rank // 8)]
    done = []
    middle = rank // 8 * 5 // 8

    each(1, low_n, lambda t: scatter(t).wait())
    mine_q = pl.ds(pl.multiple_of(low * rows_q, 8), rows_q)
    total = sq_ref[mine_q]
    for t in range(1, low_n):
        total = total + lq_ref[t]
    high = phases[1][1]
    zq_ref[high] = total

    def spread(t, owner):
        return pltpu.make_async_remote_copy(
            src_ref=zq_ref.at[owner],
            dst_ref=zq_ref.at[owner],
            send_sem=send_z.at[t],
            recv_sem=recv_z.at[t],
            device_id=phases[1][2](rem(high + t, high_n)),
            device_id_type=MESH,
        )

    each(1, high_n, lambda t: spread(t, high).start())
    eliminate(blocks, done, 0, middle)
    for s in slices:
        for k in range(n_phases):
            each(1, phases[k][0], lambda t: back(s, k, t, phases[k][1]).wait_send())

    each(1, high_n, lambda t: spread(t, high).wait_send())
    each(1, high_n, lambda t: spread(t, rem(high - t + high_n, high_n)).wait_recv())
    total = zq_ref[0]
    if high_n <= 16:
        for t in range(1, high_n):
            total = total + zq_ref[t]
    else:
        total = lax.fori_loop(1, high_n, lambda t, x: x + zq_ref[t], total)
    rq_ref[mine_q] = total / n_rep

    def gather(t, owner):
        theirs = pl.ds(pl.multiple_of(owner * rows_q, 8), rows_q)
        return pltpu.make_async_remote_copy(
            src_ref=rq_ref.at[theirs],
            dst_ref=rq_ref.at[theirs],
            send_sem=send_h.at[t],
            recv_sem=recv_h.at[t],
            device_id=(rep - low + rem(low + t, low_n), shard),
            device_id_type=MESH,
        )

    each(1, low_n, lambda t: gather(t, low).start())

    eliminate(blocks, done, middle, rank // 8)
    inverse = pltpu.roll(jnp.concatenate(done, axis=0), rank, 1)[:, :rank]
    both = jnp.concatenate([inverse, exact(inverse, inverse, TN)], axis=0)

    mom_load.wait()
    each(1, low_n, lambda t: gather(t, low).wait_send())
    each(1, low_n, lambda t: gather(t, rem(low - t + low_n, low_n)).wait_recv())

    summed = jnp.concatenate(
        [rq_ref[b * rank : (b + 1) * rank] for b in range(lane_blocks)], axis=1
    )
    both = exact(both, summed)
    right_ref[...] = both[:rank, :cols]
    mixed_ref[...] = both[rank:, :cols]


def finish(
    pair_ref, merged_ref, mixed_ref, mom_ref, right_ref,
    err_new, mom_new, query_new,
    err_ref, new_ref, sem,
):
    depth, cols = mom_ref.shape
    rank = mixed_ref.shape[0]
    half = pair_ref.shape[0]
    wide = 2 * rank
    m_high, m_low = split(mixed_ref[...])
    gap = jnp.zeros_like(m_high)
    copies = [pltpu.make_async_copy(right_ref, query_new, sem.at[0])]
    copies[0].start()
    for first, rows, on_high, on_low in (
        (0, min(half, depth), [m_high, gap, m_high, gap], [m_low, gap]),
        (half, max(0, depth - half), [gap, m_high, gap, m_high], [gap, m_low]),
    ):
        on_high = jnp.concatenate(on_high, axis=0)
        on_low = jnp.concatenate(on_low, axis=0)
        for start in range(0, rows, 256):
            size = min(256, rows - start)
            pair = pair_ref[start : start + size]
            approx = dot(pair, on_high) + dot(pair[:, :wide], on_low)
            at = slice(first + start, first + start + size)
            err_ref[at] = (merged_ref[at] - approx).astype(BF16)
            copies.append(pltpu.make_async_copy(err_ref.at[at], err_new.at[at], sem.at[len(copies)]))
            copies[-1].start()
            new_ref[at] = (0.9 * mom_ref[at].astype(F32) + approx).astype(BF16)
            copies.append(pltpu.make_async_copy(new_ref.at[at], mom_new.at[at], sem.at[len(copies)]))
            copies[-1].start()
    for copy in copies:
        copy.wait()


def step(n_rep, n_shard, activations, out_grads, error, momentum, query):
    _, depth, cols = error.shape
    rank = query.shape[1]
    tokens = activations.shape[0]
    half = up(up(-(-depth // 2), 128), 8 * n_rep * n_shard)
    core_n, mid_n, high_n = phases_of(n_rep, n_shard)
    counts = (core_n * mid_n * n_shard, high_n)
    lane_blocks = up(cols, 128) // 128
    low_n = core_n * mid_n
    rows_q = up(lane_blocks * rank, 8 * low_n) // low_n
    n_slices = 1
    sizes, size = [], half // n_slices
    for count in counts:
        size //= count
        sizes.append(size)
    dma = pltpu.SemaphoreType.DMA
    in_hbm = pl.BlockSpec(memory_space=pltpu.HBM)
    in_vmem = pl.BlockSpec(memory_space=pltpu.VMEM)
    pair, merged, mixed, right, mom = pl.pallas_call(
        functools.partial(kernel, n_rep, n_shard, rows_q, n_slices),
        out_shape=(
            jax.ShapeDtypeStruct((half, 4 * rank), BF16),
            jax.ShapeDtypeStruct((depth, cols), F32),
            jax.ShapeDtypeStruct((rank, cols), F32),
            jax.ShapeDtypeStruct((rank, cols), F32),
            jax.ShapeDtypeStruct((depth, cols), BF16),
        ),
        in_specs=[in_hbm] * 5,
        out_specs=[in_vmem] * 5,
        scratch_shapes=[
            pltpu.VMEM((2 * half, tokens), BF16),
            pltpu.VMEM((cols, tokens), BF16),
            pltpu.VMEM((2 * half, cols), BF16),
            pltpu.VMEM((rank, cols), F32),
            pltpu.VMEM((half, 2 * rank), F32),
            pltpu.VMEM((half, 2 * rank), F32),
        ]
        + [pltpu.VMEM((n_slices * c, s, 2 * rank), F32) for c, s in zip(counts, sizes)]
        + [
            pltpu.VMEM((rows_q * low_n, 128), F32),
            pltpu.VMEM((low_n, rows_q, 128), F32),
            pltpu.VMEM((high_n, rows_q, 128), F32),
            pltpu.VMEM((rows_q * low_n, 128), F32),
        ]
        + [dma((4 * n_slices + 3,))]
        + [dma((n_slices * sum(counts),))] * 4
        + [dma((low_n,))] * 2
        + [dma((high_n,))] * 2
        + [dma((low_n,))] * 2,
        compiler_params=pltpu.CompilerParams(
            collective_id=0, has_side_effects=True, vmem_limit_bytes=40 * 1024 * 1024
        ),
    )(*[pltpu.with_memory_space_constraint(x, pltpu.HBM) for x in (activations.T, out_grads.T, error.reshape(depth, cols), query.T, momentum)])
    pieces = 2 * (-(-min(half, depth) // 256) + -(-max(0, depth - half) // 256))
    err_new, mom_new, right = pl.pallas_call(
        finish,
        out_shape=(
            jax.ShapeDtypeStruct((depth, cols), BF16),
            jax.ShapeDtypeStruct((depth, cols), BF16),
            jax.ShapeDtypeStruct((rank, cols), F32),
        ),
        in_specs=[in_vmem] * 5,
        out_specs=[in_hbm] * 3,
        scratch_shapes=[
            pltpu.VMEM((depth, cols), BF16),
            pltpu.VMEM((depth, cols), BF16),
            dma((pieces + 1,)),
        ],
        compiler_params=pltpu.CompilerParams(vmem_limit_bytes=40 * 1024 * 1024),
    )(pair, merged, mixed, mom, right)
    return err_new[None], mom_new, right.T


def solution(mesh):
    return jax.shard_map(
        functools.partial(step, mesh.shape["rep"], mesh.shape["shard"]),
        mesh=mesh,
        in_specs=(
            P("rep", None),
            P("rep", "shard"),
            P("rep", None, "shard"),
            P(None, "shard"),
            P("shard", None),
        ),
        out_specs=(P("rep", None, "shard"), P(None, "shard"), P("shard", None)),
        check_vma=False,
    )
```

```python
import functools

import jax
import jax.numpy as jnp
from jax import lax
from jax.experimental import pallas as pl
from jax.experimental.pallas import tpu as pltpu
from jax.sharding import PartitionSpec as P

MESH = pl.DeviceIdType.MESH
F32 = jnp.float32
BF16 = jnp.bfloat16
NN = (((1,), (0,)), ((), ()))
NT = (((1,), (1,)), ((), ()))
TN = (((0,), (0,)), ((), ()))


def up(value, step):
    return -(-value // step) * step


def dot(a, b, dims=NN):
    return lax.dot_general(a, b, dims, preferred_element_type=F32)


def exact(a, b, dims=NN):
    return lax.dot_general(
        a, b, dims, preferred_element_type=F32, precision=lax.Precision.HIGHEST
    )


def split(x):
    high = x.astype(BF16)
    return high, (x - high.astype(F32)).astype(BF16)


def each(first, last, body):
    if last - first <= 16:
        for t in range(first, last):
            body(t)
    else:
        lax.fori_loop(first, last, lambda t, c: (body(t), c)[1], 0)


def rem(a, b):
    return lax.rem(a, jnp.int32(b))


def div(a, b):
    return lax.div(a, jnp.int32(b))


def phases_of(n_rep, n_shard):
    core = 2 if n_rep % 2 == 0 else 1
    mid = 2 if n_rep % (2 * core) == 0 else 1
    high = n_rep // (core * mid)
    return core, mid, high


def phases_here(n_rep, n_shard):
    core_n, mid_n, high_n = phases_of(n_rep, n_shard)
    rep = lax.axis_index("rep")
    shard = lax.axis_index("shard")
    core = rem(rep, core_n)
    mid = rem(div(rep, core_n), mid_n)
    high = div(rep, core_n * mid_n)
    low = core_n * mid_n
    return (
        (core_n, core, lambda d: (rep - core + d, shard)),
        (
            mid_n * n_shard,
            mid * n_shard + shard,
            lambda d: (high * low + div(d, n_shard) * core_n + core, rem(d, n_shard)),
        ),
        (high_n, high, lambda d: (d * low + mid * core_n + core, shard)),
    )


def eliminate(blocks, done, first, last):
    lanes = blocks[0].shape[1]
    sub = lax.broadcasted_iota(jnp.int32, (8, lanes), 0)
    for at in range(first, last):
        held = blocks[at:]
        cols = [
            [jnp.broadcast_to(x[:, 8 * at + k : 8 * at + k + 1], (8, lanes)) for x in held]
            for k in range(8)
        ]
        rows = [jnp.broadcast_to(held[0][k : k + 1], (8, lanes)) for k in range(8)]
        cell = [
            [jnp.broadcast_to(cols[m][0][k : k + 1], (8, lanes)) if m >= k else None for m in range(8)]
            for k in range(8)
        ]
        head = jnp.zeros((8, lanes), F32)
        for k in range(8):
            inv = 1.0 / cell[k][k]
            head = jnp.where(sub == k, rows[k] * lax.rsqrt(cell[k][k]), head)
            for m in range(k + 1, 8):
                ratio = cell[k][m] * inv
                for i in range(k + 1, m + 1):
                    cell[i][m] = cell[i][m] - cell[k][i] * ratio
                rows[m] = rows[m] - rows[k] * ratio
                for v in range(1, len(held)):
                    cols[m][v] = cols[m][v] - cols[k][v] * ratio
            scaled = rows[k] * inv
            for v in range(1, len(held)):
                held[v] = held[v] - cols[k][v] * scaled
        done.append(head)
        blocks[at + 1 :] = held[1:]


def kernel(
    n_rep, n_shard, rows_q, n_slices,
    act_hbm, out_hbm, err_hbm, query_hbm, mom_hbm,
    pair_ref, merged_ref, mixed_ref, right_ref, mom_ref,
    at_ref, gt_ref, err_ref, query_ref, part_ref, factor_ref, land0, land1, land2,
    sq_ref, lq_ref, zq_ref, rq_ref,
    in_sem, send_f, recv_f, send_g, recv_g, send_q, recv_q, send_z, recv_z, send_h, recv_h,
):
    depth, cols = err_hbm.shape
    rank = query_ref.shape[0]
    half = part_ref.shape[0]
    wide = 2 * rank
    phases = phases_here(n_rep, n_shard)
    lands = (land0, land1, land2)
    rep = lax.axis_index("rep")
    shard = lax.axis_index("shard")
    core_n, mid_n, high_n = phases_of(n_rep, n_shard)

    pieces = [(query_hbm, query_ref), (out_hbm, gt_ref)]
    part = half // n_slices
    for s in range(n_slices):
        for first in (s * part, half + s * part):
            last = min(first + part, depth)
            if first < last:
                pieces.append((err_hbm.at[first:last], err_ref.at[first:last]))
                pieces.append((act_hbm.at[first:last], at_ref.at[first:last]))
    loads = [pltpu.make_async_copy(a, b, in_sem.at[i]) for i, (a, b) in enumerate(pieces)]
    for load in loads:
        load.start()
    mom_load = pltpu.make_async_copy(mom_hbm, mom_ref, in_sem.at[len(pieces)])
    waiting = loads[2:]

    barrier = pltpu.get_barrier_semaphore()

    low_n = core_n * mid_n
    low = rem(rep, low_n)
    around = low_n * n_shard

    def greet_near(t):
        to = rem(low * n_shard + shard + t, around)
        to = (rep - low + div(to, n_shard), rem(to, n_shard))
        pl.semaphore_signal(barrier, inc=1, device_id=to, device_id_type=MESH)

    def greet_far(t):
        to = phases[2][2](rem(phases[2][1] + t, high_n))
        pl.semaphore_signal(barrier, inc=1, device_id=to, device_id_type=MESH)

    each(1, around, greet_near)
    each(1, high_n, greet_far)

    if 2 * half > depth:
        err_ref[depth:] = jnp.zeros((2 * half - depth, cols), BF16)
        at_ref[depth:] = jnp.zeros((2 * half - depth, at_ref.shape[1]), BF16)

    loads[0].wait()
    loads[1].wait()
    query = query_ref[...]
    none = jnp.zeros_like(query)
    q_top = jnp.concatenate(split(jnp.concatenate([query, none], axis=0)), axis=0)
    q_bot = jnp.concatenate(split(jnp.concatenate([none, query], axis=0)), axis=0)

    def through(q):
        gq = dot(q, gt_ref[...])
        return jnp.concatenate(split(gq[:wide] + gq[wide:]), axis=0)

    gq_top, gq_bot = through(q_top), through(q_bot)
    def rows_of(first, size):
        top = pl.ds(pl.multiple_of(first, 8 if size % 16 else 16), size)
        bot = pl.ds(pl.multiple_of(first + half, 8 if size % 16 else 16), size)
        return top, bot

    def partial(first, size):
        top, bot = rows_of(first, size)
        both = (
            dot(err_ref[top], q_top, NT) + dot(at_ref[top], gq_top, NT)
            + dot(err_ref[bot], q_bot, NT) + dot(at_ref[bot], gq_bot, NT)
        )
        part_ref[top] = both[:, :wide] + both[:, wide:]

    n_phases = len(phases)
    sems, per_slice = [], 0
    for count, _, _ in phases:
        sems.append(per_slice)
        per_slice += count
    slices = range(n_slices)
    spans = []
    for s in slices:
        base, size = s * (half // n_slices), half // n_slices
        spans.append([])
        for count, digit, _ in phases:
            size = size // count
            spans[s].append((base, size))
            base = base + digit * size

    def rows_at(s, k, owner):
        base, size = spans[s][k]
        return pl.ds(pl.multiple_of(base + owner * size, 8), size)

    def forth(s, k, t):
        count, digit, peer = phases[k]
        to = rem(digit + t, count)
        at = s * per_slice + sems[k] + t
        return pltpu.make_async_remote_copy(
            src_ref=part_ref.at[rows_at(s, k, to)],
            dst_ref=lands[k].at[s * count + t],
            send_sem=send_f.at[at],
            recv_sem=recv_f.at[at],
            device_id=peer(to),
            device_id_type=MESH,
        )

    def back(s, k, t, owner):
        count, digit, peer = phases[k]
        at = s * per_slice + sems[k] + t
        return pltpu.make_async_remote_copy(
            src_ref=factor_ref.at[rows_at(s, k, owner)],
            dst_ref=factor_ref.at[rows_at(s, k, owner)],
            send_sem=send_g.at[at],
            recv_sem=recv_g.at[at],
            device_id=peer(rem(digit + t, count)),
            device_id_type=MESH,
        )

    def send_forth(s, k):
        each(1, phases[k][0], lambda t: forth(s, k, t).start())

    def add_up(s, k):
        count, digit, _ = phases[k]
        each(1, count, lambda t: forth(s, k, t).wait())
        mine = rows_at(s, k, digit)
        total = part_ref[mine]
        land = lands[k]
        if count <= 16:
            for t in range(1, count):
                total = total + land[s * count + t]
        else:
            total = lax.fori_loop(1, count, lambda t, x: x + land[s * count + t], total)
        if k < n_phases - 1:
            part_ref[mine] = total
        else:
            factor_ref[mine] = total

    def send_back(s, k):
        each(1, phases[k][0], lambda t: back(s, k, t, phases[k][1]).start())

    def arrive(s, k):
        count, digit, _ = phases[k]
        each(1, count, lambda t: back(s, k, t, rem(digit - t + count, count)).wait_recv())

    count, digit, _ = phases[0]
    for s in slices:
        base, size = spans[s][0]
        for load in waiting[4 * s : 4 * s + 4] if s < n_slices - 1 else waiting[4 * s :]:
            load.wait()
        for t in range(1, count):
            partial(base + rem(digit + t, count) * size, size)
        if s == 0:
            pl.semaphore_wait(barrier, around - 1 + high_n - 1)
        send_forth(s, 0)
        if s > 0:
            add_up(s - 1, 0)
            send_forth(s - 1, 1)
        partial(base + digit * size, size)
    add_up(n_slices - 1, 0)
    send_forth(n_slices - 1, 1)
    mom_load.start()
    for k in range(1, n_phases):
        if k > 1:
            for s in slices:
                add_up(s, k - 1)
                send_forth(s, k)
        if k == 1:
            for first in range(0, depth, 512):
                last = min(first + 512, depth)
                merged_ref[first:last] = dot(
                    at_ref[first:last], gt_ref[...], NT
                ) + err_ref[first:last].astype(F32)
    for s in slices:
        add_up(s, n_phases - 1)
        send_back(s, n_phases - 1)

    af, local, halves = [], [], []

    def use(first, size):
        top, bot = rows_of(first, size)
        pair = jnp.concatenate(split(factor_ref[top]), axis=1)
        pair_ref[top] = pair
        pair_t = pair.T
        ft_top = jnp.concatenate([pair_t[:rank], pair_t[wide : wide + rank]], axis=0)
        ft_bot = jnp.concatenate([pair_t[rank:wide], pair_t[wide + rank :]], axis=0)
        af.append(dot(ft_top, at_ref[top]) + dot(ft_bot, at_ref[bot]))
        local.append(dot(ft_top, err_ref[top]) + dot(ft_bot, err_ref[bot]))
        halves.append((pair_t, pair))

    for k in range(n_phases - 1, 0, -1):
        for s in slices:
            arrive(s, k)
            send_back(s, k - 1)
            if k == 1:
                base, size = spans[s][0]
                use(base + digit * size, size)
    for s in slices:
        arrive(s, 0)
        base, size = spans[s][0]
        for t in range(1, count):
            use(base + rem(digit - t + count, count) * size, size)

    af = sum(af[1:], af[0])
    local = sum(local[1:], local[0])
    af = jnp.concatenate(split(af[:rank] + af[rank:]), axis=0)
    local = local + dot(af, gt_ref[...], NT)
    local = local[:rank] + local[rank:]
    lane_blocks = up(cols, 128) // 128
    for b in range(lane_blocks):
        here = min(128, cols - 128 * b)
        sq_ref[b * rank : (b + 1) * rank, :here] = local[:, 128 * b : 128 * b + here]
        if here < 128:
            sq_ref[b * rank : (b + 1) * rank, here:] = jnp.zeros((rank, 128 - here), F32)
    if sq_ref.shape[0] > lane_blocks * rank:
        sq_ref[lane_blocks * rank :] = jnp.zeros((sq_ref.shape[0] - lane_blocks * rank, 128), F32)

    def scatter(t):
        to = rem(low + t, low_n)
        return pltpu.make_async_remote_copy(
            src_ref=sq_ref.at[pl.ds(pl.multiple_of(to * rows_q, 8), rows_q)],
            dst_ref=lq_ref.at[t],
            send_sem=send_q.at[t],
            recv_sem=recv_q.at[t],
            device_id=(rep - low + to, shard),
            device_id_type=MESH,
        )

    each(1, low_n, lambda t: scatter(t).start())

    prod = sum([dot(x, y) for x, y in halves[1:]], dot(*halves[0]))
    g1 = prod[:rank] + prod[wide : wide + rank]
    g2 = prod[rank:wide] + prod[wide + rank :]
    g1 = g1[:, :wide] + g1[:, wide:]
    g2 = g2[:, :wide] + g2[:, wide:]
    gram = g1 + pltpu.roll(g2, rank, 1)
    lane = lax.broadcasted_iota(jnp.int32, (rank, wide), 1)
    row = lax.broadcasted_iota(jnp.int32, (rank, wide), 0)
    aug = jnp.where(lane < rank, gram, jnp.where(lane - rank == row, 1.0, 0.0))
    blocks = [aug[8 * v : 8 * v + 8] for v in range(rank // 8)]
    done = []
    middle = rank // 8 * 5 // 8
    eliminate(blocks, done, 0, 1)

    each(1, low_n, lambda t: scatter(t).wait())
    mine_q = pl.ds(pl.multiple_of(low * rows_q, 8), rows_q)
    total = sq_ref[mine_q]
    for t in range(1, low_n):
        total = total + lq_ref[t]
    high = phases[2][1]
    zq_ref[high] = total

    def spread(t, owner):
        return pltpu.make_async_remote_copy(
            src_ref=zq_ref.at[owner],
            dst_ref=zq_ref.at[owner],
            send_sem=send_z.at[t],
            recv_sem=recv_z.at[t],
            device_id=phases[2][2](rem(high + t, high_n)),
            device_id_type=MESH,
        )

    each(1, high_n, lambda t: spread(t, high).start())
    eliminate(blocks, done, 1, middle)
    for s in slices:
        for k in range(n_phases):
            each(1, phases[k][0], lambda t: back(s, k, t, phases[k][1]).wait_send())

    each(1, high_n, lambda t: spread(t, high).wait_send())
    each(1, high_n, lambda t: spread(t, rem(high - t + high_n, high_n)).wait_recv())
    total = zq_ref[0]
    if high_n <= 16:
        for t in range(1, high_n):
            total = total + zq_ref[t]
    else:
        total = lax.fori_loop(1, high_n, lambda t, x: x + zq_ref[t], total)
    rq_ref[mine_q] = total / n_rep

    def gather(t, owner):
        theirs = pl.ds(pl.multiple_of(owner * rows_q, 8), rows_q)
        return pltpu.make_async_remote_copy(
            src_ref=rq_ref.at[theirs],
            dst_ref=rq_ref.at[theirs],
            send_sem=send_h.at[t],
            recv_sem=recv_h.at[t],
            device_id=(rep - low + rem(low + t, low_n), shard),
            device_id_type=MESH,
        )

    each(1, low_n, lambda t: gather(t, low).start())

    eliminate(blocks, done, middle, rank // 8)
    inverse = pltpu.roll(jnp.concatenate(done, axis=0), rank, 1)[:, :rank]
    both = jnp.concatenate([inverse, exact(inverse, inverse, TN)], axis=0)

    mom_load.wait()
    each(1, low_n, lambda t: gather(t, low).wait_send())
    each(1, low_n, lambda t: gather(t, rem(low - t + low_n, low_n)).wait_recv())

    summed = jnp.concatenate(
        [rq_ref[b * rank : (b + 1) * rank] for b in range(lane_blocks)], axis=1
    )
    both = exact(both, summed)
    right_ref[...] = both[:rank, :cols]
    mixed_ref[...] = both[rank:, :cols]


def finish(
    pair_ref, merged_ref, mixed_ref, mom_ref, right_ref,
    err_new, mom_new, query_new,
    err_ref, new_ref, sem,
):
    depth, cols = mom_ref.shape
    rank = mixed_ref.shape[0]
    half = pair_ref.shape[0]
    wide = 2 * rank
    m_high, m_low = split(mixed_ref[...])
    gap = jnp.zeros_like(m_high)
    copies = [pltpu.make_async_copy(right_ref, query_new, sem.at[0])]
    copies[0].start()
    for first, rows, on_high, on_low in (
        (0, min(half, depth), [m_high, gap, m_high, gap], [m_low, gap]),
        (half, max(0, depth - half), [gap, m_high, gap, m_high], [gap, m_low]),
    ):
        on_high = jnp.concatenate(on_high, axis=0)
        on_low = jnp.concatenate(on_low, axis=0)
        for start in range(0, rows, 256):
            size = min(256, rows - start)
            pair = pair_ref[start : start + size]
            approx = dot(pair, on_high) + dot(pair[:, :wide], on_low)
            at = slice(first + start, first + start + size)
            err_ref[at] = (merged_ref[at] - approx).astype(BF16)
            copies.append(pltpu.make_async_copy(err_ref.at[at], err_new.at[at], sem.at[len(copies)]))
            copies[-1].start()
            new_ref[at] = (0.9 * mom_ref[at].astype(F32) + approx).astype(BF16)
            copies.append(pltpu.make_async_copy(new_ref.at[at], mom_new.at[at], sem.at[len(copies)]))
            copies[-1].start()
    for copy in copies:
        copy.wait()


def step(n_rep, n_shard, activations, out_grads, error, momentum, query):
    _, depth, cols = error.shape
    rank = query.shape[1]
    tokens = activations.shape[0]
    half = up(up(-(-depth // 2), 128), 8 * n_rep * n_shard)
    core_n, mid_n, high_n = phases_of(n_rep, n_shard)
    counts = (core_n, mid_n * n_shard, high_n)
    lane_blocks = up(cols, 128) // 128
    low_n = core_n * mid_n
    rows_q = up(lane_blocks * rank, 8 * low_n) // low_n
    n_slices = 2 if half // (8 * n_rep * n_shard) % 2 == 0 else 1
    sizes, size = [], half // n_slices
    for count in counts:
        size //= count
        sizes.append(size)
    dma = pltpu.SemaphoreType.DMA
    in_hbm = pl.BlockSpec(memory_space=pltpu.HBM)
    in_vmem = pl.BlockSpec(memory_space=pltpu.VMEM)
    pair, merged, mixed, right, mom = pl.pallas_call(
        functools.partial(kernel, n_rep, n_shard, rows_q, n_slices),
        out_shape=(
            jax.ShapeDtypeStruct((half, 4 * rank), BF16),
            jax.ShapeDtypeStruct((depth, cols), F32),
            jax.ShapeDtypeStruct((rank, cols), F32),
            jax.ShapeDtypeStruct((rank, cols), F32),
            jax.ShapeDtypeStruct((depth, cols), BF16),
        ),
        in_specs=[in_hbm] * 5,
        out_specs=[in_vmem] * 5,
        scratch_shapes=[
            pltpu.VMEM((2 * half, tokens), BF16),
            pltpu.VMEM((cols, tokens), BF16),
            pltpu.VMEM((2 * half, cols), BF16),
            pltpu.VMEM((rank, cols), F32),
            pltpu.VMEM((half, 2 * rank), F32),
            pltpu.VMEM((half, 2 * rank), F32),
        ]
        + [pltpu.VMEM((n_slices * c, s, 2 * rank), F32) for c, s in zip(counts, sizes)]
        + [
            pltpu.VMEM((rows_q * low_n, 128), F32),
            pltpu.VMEM((low_n, rows_q, 128), F32),
            pltpu.VMEM((high_n, rows_q, 128), F32),
            pltpu.VMEM((rows_q * low_n, 128), F32),
        ]
        + [dma((4 * n_slices + 3,))]
        + [dma((n_slices * sum(counts),))] * 4
        + [dma((low_n,))] * 2
        + [dma((high_n,))] * 2
        + [dma((low_n,))] * 2,
        compiler_params=pltpu.CompilerParams(
            collective_id=0, has_side_effects=True, vmem_limit_bytes=40 * 1024 * 1024
        ),
    )(*[pltpu.with_memory_space_constraint(x, pltpu.HBM) for x in (activations.T, out_grads.T, error.reshape(depth, cols), query.T, momentum)])
    pieces = 2 * (-(-min(half, depth) // 256) + -(-max(0, depth - half) // 256))
    err_new, mom_new, right = pl.pallas_call(
        finish,
        out_shape=(
            jax.ShapeDtypeStruct((depth, cols), BF16),
            jax.ShapeDtypeStruct((depth, cols), BF16),
            jax.ShapeDtypeStruct((rank, cols), F32),
        ),
        in_specs=[in_vmem] * 5,
        out_specs=[in_hbm] * 3,
        scratch_shapes=[
            pltpu.VMEM((depth, cols), BF16),
            pltpu.VMEM((depth, cols), BF16),
            dma((pieces + 1,)),
        ],
        compiler_params=pltpu.CompilerParams(vmem_limit_bytes=40 * 1024 * 1024),
    )(pair, merged, mixed, mom, right)
    return err_new[None], mom_new, right.T


def solution(mesh):
    return jax.shard_map(
        functools.partial(step, mesh.shape["rep"], mesh.shape["shard"]),
        mesh=mesh,
        in_specs=(
            P("rep", None),
            P("rep", "shard"),
            P("rep", None, "shard"),
            P(None, "shard"),
            P("shard", None),
        ),
        out_specs=(P("rep", None, "shard"), P(None, "shard"), P("shard", None)),
        check_vma=False,
    )
```

```python
import functools

import jax
import jax.numpy as jnp
from jax import lax
from jax.experimental import pallas as pl
from jax.experimental.pallas import tpu as pltpu
from jax.sharding import PartitionSpec as P

MESH = pl.DeviceIdType.MESH
F32 = jnp.float32
BF16 = jnp.bfloat16
NN = (((1,), (0,)), ((), ()))
NT = (((1,), (1,)), ((), ()))
TN = (((0,), (0,)), ((), ()))


def up(value, step):
    return -(-value // step) * step


def dot(a, b, dims=NN):
    return lax.dot_general(a, b, dims, preferred_element_type=F32)


def exact(a, b, dims=NN):
    return lax.dot_general(
        a, b, dims, preferred_element_type=F32, precision=lax.Precision.HIGHEST
    )


def split(x):
    high = x.astype(BF16)
    return high, (x - high.astype(F32)).astype(BF16)


def each(first, last, body):
    if last - first <= 16:
        for t in range(first, last):
            body(t)
    else:
        lax.fori_loop(first, last, lambda t, c: (body(t), c)[1], 0)


def rem(a, b):
    return lax.rem(a, jnp.int32(b))


def div(a, b):
    return lax.div(a, jnp.int32(b))


def phases_of(n_rep, n_shard):
    core = 2 if n_rep % 2 == 0 else 1
    mid = 2 if n_rep % (2 * core) == 0 else 1
    high = n_rep // (core * mid)
    return core, mid, high


def near_of(high_n):
    return 1


def phases_here(n_rep, n_shard):
    core_n, mid_n, high_n = phases_of(n_rep, n_shard)
    near_n = near_of(high_n)
    rep = lax.axis_index("rep")
    shard = lax.axis_index("shard")
    core = rem(rep, core_n)
    mid = rem(div(rep, core_n), mid_n)
    high = div(rep, core_n * mid_n)
    low = core_n * mid_n
    return (
        (core_n, core, lambda d: (rep - core + d, shard)),
        (
            mid_n * n_shard,
            mid * n_shard + shard,
            lambda d: (high * low + div(d, n_shard) * core_n + core, rem(d, n_shard)),
        ),
        (
            near_n,
            rem(high, near_n),
            lambda d: ((high - rem(high, near_n) + d) * low + mid * core_n + core, shard),
        ),
    ), (high_n, high, lambda d: (d * low + mid * core_n + core, shard)), (
        high_n // near_n,
        div(high, near_n),
        lambda d: ((d * near_n + rem(high, near_n)) * low + mid * core_n + core, shard),
    )


def eliminate(blocks, done, first, last):
    lanes = blocks[0].shape[1]
    sub = lax.broadcasted_iota(jnp.int32, (8, lanes), 0)
    for at in range(first, last):
        held = blocks[at:]
        cols = [
            [jnp.broadcast_to(x[:, 8 * at + k : 8 * at + k + 1], (8, lanes)) for x in held]
            for k in range(8)
        ]
        rows = [jnp.broadcast_to(held[0][k : k + 1], (8, lanes)) for k in range(8)]
        cell = [
            [jnp.broadcast_to(cols[m][0][k : k + 1], (8, lanes)) if m >= k else None for m in range(8)]
            for k in range(8)
        ]
        head = jnp.zeros((8, lanes), F32)
        for k in range(8):
            inv = 1.0 / cell[k][k]
            head = jnp.where(sub == k, rows[k] * lax.rsqrt(cell[k][k]), head)
            for m in range(k + 1, 8):
                ratio = cell[k][m] * inv
                for i in range(k + 1, m + 1):
                    cell[i][m] = cell[i][m] - cell[k][i] * ratio
                rows[m] = rows[m] - rows[k] * ratio
                for v in range(1, len(held)):
                    cols[m][v] = cols[m][v] - cols[k][v] * ratio
            scaled = rows[k] * inv
            for v in range(1, len(held)):
                held[v] = held[v] - cols[k][v] * scaled
        done.append(head)
        blocks[at + 1 :] = held[1:]


def kernel(
    n_rep, n_shard, rows_q, n_slices,
    act_hbm, out_hbm, err_hbm, query_hbm, mom_hbm,
    pair_ref, merged_ref, mixed_ref, right_ref, mom_ref,
    at_ref, gt_ref, err_ref, query_ref, part_ref, factor_ref, land0, land1, land2, ex_ref,
    sq_ref, lq_ref, zq_ref, rq_ref,
    in_sem, send_f, recv_f, send_g, recv_g, send_q, recv_q, send_z, recv_z, send_h, recv_h, send_x, recv_x,
):
    depth, cols = err_hbm.shape
    rank = query_ref.shape[0]
    half = part_ref.shape[0]
    wide = 2 * rank
    phases, far, cross = phases_here(n_rep, n_shard)
    lands = (land0, land1, land2)
    rep = lax.axis_index("rep")
    shard = lax.axis_index("shard")
    core_n, mid_n, high_n = phases_of(n_rep, n_shard)

    pieces = [(query_hbm, query_ref), (out_hbm, gt_ref)]
    part = half // n_slices
    for s in range(n_slices):
        for first in (s * part, half + s * part):
            last = min(first + part, depth)
            if first < last:
                pieces.append((err_hbm.at[first:last], err_ref.at[first:last]))
                pieces.append((act_hbm.at[first:last], at_ref.at[first:last]))
    loads = [pltpu.make_async_copy(a, b, in_sem.at[i]) for i, (a, b) in enumerate(pieces)]
    for load in loads:
        load.start()
    mom_load = pltpu.make_async_copy(mom_hbm, mom_ref, in_sem.at[len(pieces)])
    waiting = loads[2:]

    barrier = pltpu.get_barrier_semaphore()

    low_n = core_n * mid_n
    low = rem(rep, low_n)
    around = low_n * n_shard

    def greet_near(t):
        to = rem(low * n_shard + shard + t, around)
        to = (rep - low + div(to, n_shard), rem(to, n_shard))
        pl.semaphore_signal(barrier, inc=1, device_id=to, device_id_type=MESH)

    def greet_far(t):
        to = far[2](rem(far[1] + t, high_n))
        pl.semaphore_signal(barrier, inc=1, device_id=to, device_id_type=MESH)

    each(1, around, greet_near)
    each(1, high_n, greet_far)

    if 2 * half > depth:
        err_ref[depth:] = jnp.zeros((2 * half - depth, cols), BF16)
        at_ref[depth:] = jnp.zeros((2 * half - depth, at_ref.shape[1]), BF16)

    loads[0].wait()
    loads[1].wait()
    query = query_ref[...]
    none = jnp.zeros_like(query)
    q_top = jnp.concatenate(split(jnp.concatenate([query, none], axis=0)), axis=0)
    q_bot = jnp.concatenate(split(jnp.concatenate([none, query], axis=0)), axis=0)

    def through(q):
        gq = dot(q, gt_ref[...])
        return jnp.concatenate(split(gq[:wide] + gq[wide:]), axis=0)

    gq_top, gq_bot = through(q_top), through(q_bot)
    def rows_of(first, size):
        top = pl.ds(pl.multiple_of(first, 8 if size % 16 else 16), size)
        bot = pl.ds(pl.multiple_of(first + half, 8 if size % 16 else 16), size)
        return top, bot

    def partial(first, size):
        top, bot = rows_of(first, size)
        both = (
            dot(err_ref[top], q_top, NT) + dot(at_ref[top], gq_top, NT)
            + dot(err_ref[bot], q_bot, NT) + dot(at_ref[bot], gq_bot, NT)
        )
        part_ref[top] = both[:, :wide] + both[:, wide:]

    n_phases = len(phases)
    sems, per_slice = [], 0
    for count, _, _ in phases:
        sems.append(per_slice)
        per_slice += count
    slices = range(n_slices)
    spans = []
    for s in slices:
        base, size = s * (half // n_slices), half // n_slices
        spans.append([])
        for count, digit, _ in phases:
            size = size // count
            spans[s].append((base, size))
            base = base + digit * size

    def rows_at(s, k, owner):
        base, size = spans[s][k]
        return pl.ds(pl.multiple_of(base + owner * size, 8), size)

    def forth(s, k, t):
        count, digit, peer = phases[k]
        to = rem(digit + t, count)
        at = s * per_slice + sems[k] + t
        return pltpu.make_async_remote_copy(
            src_ref=part_ref.at[rows_at(s, k, to)],
            dst_ref=lands[k].at[s * count + t],
            send_sem=send_f.at[at],
            recv_sem=recv_f.at[at],
            device_id=peer(to),
            device_id_type=MESH,
        )

    def back(s, k, t, owner):
        count, digit, peer = phases[k]
        at = s * per_slice + sems[k] + t
        return pltpu.make_async_remote_copy(
            src_ref=factor_ref.at[rows_at(s, k, owner)],
            dst_ref=factor_ref.at[rows_at(s, k, owner)],
            send_sem=send_g.at[at],
            recv_sem=recv_g.at[at],
            device_id=peer(rem(digit + t, count)),
            device_id_type=MESH,
        )

    def send_forth(s, k):
        each(1, phases[k][0], lambda t: forth(s, k, t).start())

    def add_up(s, k):
        count, digit, _ = phases[k]
        each(1, count, lambda t: forth(s, k, t).wait())
        mine = rows_at(s, k, digit)
        total = part_ref[mine]
        land = lands[k]
        if count <= 16:
            for t in range(1, count):
                total = total + land[s * count + t]
        else:
            total = lax.fori_loop(1, count, lambda t, x: x + land[s * count + t], total)
        if k < n_phases - 1:
            part_ref[mine] = total
        else:
            ex_ref[s * cross[0] + cross[1]] = total

    def swap(s, t, owner):
        count, digit, peer = cross
        return pltpu.make_async_remote_copy(
            src_ref=ex_ref.at[s * count + owner],
            dst_ref=ex_ref.at[s * count + owner],
            send_sem=send_x.at[s * count + t],
            recv_sem=recv_x.at[s * count + t],
            device_id=peer(rem(digit + t, count)),
            device_id_type=MESH,
        )

    def send_back(s, k):
        each(1, phases[k][0], lambda t: back(s, k, t, phases[k][1]).start())

    def arrive(s, k):
        count, digit, _ = phases[k]
        each(1, count, lambda t: back(s, k, t, rem(digit - t + count, count)).wait_recv())

    count, digit, _ = phases[0]
    for s in slices:
        base, size = spans[s][0]
        for load in waiting[4 * s : 4 * s + 4] if s < n_slices - 1 else waiting[4 * s :]:
            load.wait()
        for t in range(1, count):
            partial(base + rem(digit + t, count) * size, size)
        if s == 0:
            pl.semaphore_wait(barrier, around - 1 + high_n - 1)
        send_forth(s, 0)
        if s > 0:
            add_up(s - 1, 0)
            send_forth(s - 1, 1)
        partial(base + digit * size, size)
    add_up(n_slices - 1, 0)
    send_forth(n_slices - 1, 1)
    mom_load.start()
    for k in range(1, n_phases):
        if k > 1:
            for s in slices:
                add_up(s, k - 1)
                send_forth(s, k)
        if k == 1:
            for first in range(0, depth, 512):
                last = min(first + 512, depth)
                merged_ref[first:last] = dot(
                    at_ref[first:last], gt_ref[...], NT
                ) + err_ref[first:last].astype(F32)
    for s in slices:
        add_up(s, n_phases - 1)
        each(1, cross[0], lambda t: swap(s, t, cross[1]).start())
    for s in slices:
        n, digit, _ = cross
        each(1, n, lambda t: swap(s, t, rem(digit - t + n, n)).wait_recv())
        total = ex_ref[s * n]
        if n <= 16:
            for t in range(1, n):
                total = total + ex_ref[s * n + t]
        else:
            total = lax.fori_loop(1, n, lambda t, x: x + ex_ref[s * n + t], total)
        factor_ref[rows_at(s, n_phases - 1, phases[-1][1])] = total
        send_back(s, n_phases - 1)
    count, digit, _ = phases[0]

    af, local, halves = [], [], []

    def use(first, size):
        top, bot = rows_of(first, size)
        pair = jnp.concatenate(split(factor_ref[top]), axis=1)
        pair_ref[top] = pair
        pair_t = pair.T
        ft_top = jnp.concatenate([pair_t[:rank], pair_t[wide : wide + rank]], axis=0)
        ft_bot = jnp.concatenate([pair_t[rank:wide], pair_t[wide + rank :]], axis=0)
        af.append(dot(ft_top, at_ref[top]) + dot(ft_bot, at_ref[bot]))
        local.append(dot(ft_top, err_ref[top]) + dot(ft_bot, err_ref[bot]))
        halves.append((pair_t, pair))

    for k in range(n_phases - 1, 0, -1):
        for s in slices:
            arrive(s, k)
            send_back(s, k - 1)
            if k == 1:
                base, size = spans[s][0]
                use(base + digit * size, size)
    for s in slices:
        arrive(s, 0)
        base, size = spans[s][0]
        for t in range(1, count):
            use(base + rem(digit - t + count, count) * size, size)

    af = sum(af[1:], af[0])
    local = sum(local[1:], local[0])
    af = jnp.concatenate(split(af[:rank] + af[rank:]), axis=0)
    local = local + dot(af, gt_ref[...], NT)
    local = local[:rank] + local[rank:]
    lane_blocks = up(cols, 128) // 128
    for b in range(lane_blocks):
        here = min(128, cols - 128 * b)
        sq_ref[b * rank : (b + 1) * rank, :here] = local[:, 128 * b : 128 * b + here]
        if here < 128:
            sq_ref[b * rank : (b + 1) * rank, here:] = jnp.zeros((rank, 128 - here), F32)
    if sq_ref.shape[0] > lane_blocks * rank:
        sq_ref[lane_blocks * rank :] = jnp.zeros((sq_ref.shape[0] - lane_blocks * rank, 128), F32)

    def scatter(t):
        to = rem(low + t, low_n)
        return pltpu.make_async_remote_copy(
            src_ref=sq_ref.at[pl.ds(pl.multiple_of(to * rows_q, 8), rows_q)],
            dst_ref=lq_ref.at[t],
            send_sem=send_q.at[t],
            recv_sem=recv_q.at[t],
            device_id=(rep - low + to, shard),
            device_id_type=MESH,
        )

    each(1, low_n, lambda t: scatter(t).start())

    prod = sum([dot(x, y) for x, y in halves[1:]], dot(*halves[0]))
    g1 = prod[:rank] + prod[wide : wide + rank]
    g2 = prod[rank:wide] + prod[wide + rank :]
    g1 = g1[:, :wide] + g1[:, wide:]
    g2 = g2[:, :wide] + g2[:, wide:]
    gram = g1 + pltpu.roll(g2, rank, 1)
    lane = lax.broadcasted_iota(jnp.int32, (rank, wide), 1)
    row = lax.broadcasted_iota(jnp.int32, (rank, wide), 0)
    aug = jnp.where(lane < rank, gram, jnp.where(lane - rank == row, 1.0, 0.0))
    blocks = [aug[8 * v : 8 * v + 8] for v in range(rank // 8)]
    done = []
    middle = rank // 8 * 5 // 8
    eliminate(blocks, done, 0, 1)

    each(1, low_n, lambda t: scatter(t).wait())
    mine_q = pl.ds(pl.multiple_of(low * rows_q, 8), rows_q)
    total = sq_ref[mine_q]
    for t in range(1, low_n):
        total = total + lq_ref[t]
    high = far[1]
    zq_ref[high] = total

    def spread(t, owner):
        return pltpu.make_async_remote_copy(
            src_ref=zq_ref.at[owner],
            dst_ref=zq_ref.at[owner],
            send_sem=send_z.at[t],
            recv_sem=recv_z.at[t],
            device_id=far[2](rem(high + t, high_n)),
            device_id_type=MESH,
        )

    each(1, high_n, lambda t: spread(t, high).start())
    eliminate(blocks, done, 1, middle)
    for s in slices:
        for k in range(n_phases):
            each(1, phases[k][0], lambda t: back(s, k, t, phases[k][1]).wait_send())
        each(1, cross[0], lambda t: swap(s, t, cross[1]).wait_send())

    each(1, high_n, lambda t: spread(t, high).wait_send())
    each(1, high_n, lambda t: spread(t, rem(high - t + high_n, high_n)).wait_recv())
    total = zq_ref[0]
    if high_n <= 16:
        for t in range(1, high_n):
            total = total + zq_ref[t]
    else:
        total = lax.fori_loop(1, high_n, lambda t, x: x + zq_ref[t], total)
    rq_ref[mine_q] = total / n_rep

    def gather(t, owner):
        theirs = pl.ds(pl.multiple_of(owner * rows_q, 8), rows_q)
        return pltpu.make_async_remote_copy(
            src_ref=rq_ref.at[theirs],
            dst_ref=rq_ref.at[theirs],
            send_sem=send_h.at[t],
            recv_sem=recv_h.at[t],
            device_id=(rep - low + rem(low + t, low_n), shard),
            device_id_type=MESH,
        )

    each(1, low_n, lambda t: gather(t, low).start())

    eliminate(blocks, done, middle, rank // 8)
    inverse = pltpu.roll(jnp.concatenate(done, axis=0), rank, 1)[:, :rank]
    both = jnp.concatenate([inverse, exact(inverse, inverse, TN)], axis=0)

    mom_load.wait()
    each(1, low_n, lambda t: gather(t, low).wait_send())
    each(1, low_n, lambda t: gather(t, rem(low - t + low_n, low_n)).wait_recv())

    summed = jnp.concatenate(
        [rq_ref[b * rank : (b + 1) * rank] for b in range(lane_blocks)], axis=1
    )
    both = exact(both, summed)
    right_ref[...] = both[:rank, :cols]
    mixed_ref[...] = both[rank:, :cols]


def finish(
    pair_ref, merged_ref, mixed_ref, mom_ref, right_ref,
    err_new, mom_new, query_new,
    err_ref, new_ref, sem,
):
    depth, cols = mom_ref.shape
    rank = mixed_ref.shape[0]
    half = pair_ref.shape[0]
    wide = 2 * rank
    m_high, m_low = split(mixed_ref[...])
    gap = jnp.zeros_like(m_high)
    copies = [pltpu.make_async_copy(right_ref, query_new, sem.at[0])]
    copies[0].start()
    for first, rows, on_high, on_low in (
        (0, min(half, depth), [m_high, gap, m_high, gap], [m_low, gap]),
        (half, max(0, depth - half), [gap, m_high, gap, m_high], [gap, m_low]),
    ):
        on_high = jnp.concatenate(on_high, axis=0)
        on_low = jnp.concatenate(on_low, axis=0)
        for start in range(0, rows, 256):
            size = min(256, rows - start)
            pair = pair_ref[start : start + size]
            approx = dot(pair, on_high) + dot(pair[:, :wide], on_low)
            at = slice(first + start, first + start + size)
            err_ref[at] = (merged_ref[at] - approx).astype(BF16)
            copies.append(pltpu.make_async_copy(err_ref.at[at], err_new.at[at], sem.at[len(copies)]))
            copies[-1].start()
            new_ref[at] = (0.9 * mom_ref[at].astype(F32) + approx).astype(BF16)
            copies.append(pltpu.make_async_copy(new_ref.at[at], mom_new.at[at], sem.at[len(copies)]))
            copies[-1].start()
    for copy in copies:
        copy.wait()


def step(n_rep, n_shard, activations, out_grads, error, momentum, query):
    _, depth, cols = error.shape
    rank = query.shape[1]
    tokens = activations.shape[0]
    half = up(up(-(-depth // 2), 128), 8 * n_rep * n_shard)
    core_n, mid_n, high_n = phases_of(n_rep, n_shard)
    near_n = near_of(high_n)
    counts = (core_n, mid_n * n_shard, near_n)
    n_cross = high_n // near_n
    lane_blocks = up(cols, 128) // 128
    low_n = core_n * mid_n
    rows_q = up(lane_blocks * rank, 8 * low_n) // low_n
    n_slices = 2 if half // (8 * n_rep * n_shard) % 2 == 0 else 1
    sizes, size = [], half // n_slices
    for count in counts:
        size //= count
        sizes.append(size)
    dma = pltpu.SemaphoreType.DMA
    in_hbm = pl.BlockSpec(memory_space=pltpu.HBM)
    in_vmem = pl.BlockSpec(memory_space=pltpu.VMEM)
    pair, merged, mixed, right, mom = pl.pallas_call(
        functools.partial(kernel, n_rep, n_shard, rows_q, n_slices),
        out_shape=(
            jax.ShapeDtypeStruct((half, 4 * rank), BF16),
            jax.ShapeDtypeStruct((depth, cols), F32),
            jax.ShapeDtypeStruct((rank, cols), F32),
            jax.ShapeDtypeStruct((rank, cols), F32),
            jax.ShapeDtypeStruct((depth, cols), BF16),
        ),
        in_specs=[in_hbm] * 5,
        out_specs=[in_vmem] * 5,
        scratch_shapes=[
            pltpu.VMEM((2 * half, tokens), BF16),
            pltpu.VMEM((cols, tokens), BF16),
            pltpu.VMEM((2 * half, cols), BF16),
            pltpu.VMEM((rank, cols), F32),
            pltpu.VMEM((half, 2 * rank), F32),
            pltpu.VMEM((half, 2 * rank), F32),
        ]
        + [pltpu.VMEM((n_slices * c, s, 2 * rank), F32) for c, s in zip(counts, sizes)]
        + [
            pltpu.VMEM((n_slices * n_cross, sizes[-1], 2 * rank), F32),
            pltpu.VMEM((rows_q * low_n, 128), F32),
            pltpu.VMEM((low_n, rows_q, 128), F32),
            pltpu.VMEM((high_n, rows_q, 128), F32),
            pltpu.VMEM((rows_q * low_n, 128), F32),
        ]
        + [dma((4 * n_slices + 3,))]
        + [dma((n_slices * sum(counts),))] * 4
        + [dma((low_n,))] * 2
        + [dma((high_n,))] * 2
        + [dma((low_n,))] * 2
        + [dma((n_slices * n_cross,))] * 2,
        compiler_params=pltpu.CompilerParams(
            collective_id=0, has_side_effects=True, vmem_limit_bytes=40 * 1024 * 1024
        ),
    )(*[pltpu.with_memory_space_constraint(x, pltpu.HBM) for x in (activations.T, out_grads.T, error.reshape(depth, cols), query.T, momentum)])
    pieces = 2 * (-(-min(half, depth) // 256) + -(-max(0, depth - half) // 256))
    err_new, mom_new, right = pl.pallas_call(
        finish,
        out_shape=(
            jax.ShapeDtypeStruct((depth, cols), BF16),
            jax.ShapeDtypeStruct((depth, cols), BF16),
            jax.ShapeDtypeStruct((rank, cols), F32),
        ),
        in_specs=[in_vmem] * 5,
        out_specs=[in_hbm] * 3,
        scratch_shapes=[
            pltpu.VMEM((depth, cols), BF16),
            pltpu.VMEM((depth, cols), BF16),
            dma((pieces + 1,)),
        ],
        compiler_params=pltpu.CompilerParams(vmem_limit_bytes=40 * 1024 * 1024),
    )(pair, merged, mixed, mom, right)
    return err_new[None], mom_new, right.T


def solution(mesh):
    return jax.shard_map(
        functools.partial(step, mesh.shape["rep"], mesh.shape["shard"]),
        mesh=mesh,
        in_specs=(
            P("rep", None),
            P("rep", "shard"),
            P("rep", None, "shard"),
            P(None, "shard"),
            P("shard", None),
        ),
        out_specs=(P("rep", None, "shard"), P(None, "shard"), P("shard", None)),
        check_vma=False,
    )
```
